512 devices in a mesh: fit: 32 (over y_lo, z), pair: 16 (over x, y_hi, core).
Axes of the slice: x: 4, y: 8 (y_hi: 2, y_lo: 4; y = y_hi * 4 + y_lo), z: 8, core: 2. Of those that a mesh axis runs over, the one named last changes fastest.
Arguments:
- left_factors: bfloat16 [8000, 2048], P('fit'), may hold values from -0.6328125 to 0.6328125
- right_factors: bfloat16 [4, 8000, 2048], P(None, 'fit', 'pair'), may hold values from -0.6328125 to 0.6328125
- virtual_energy: float32 [2048], replicated, may hold values from 0.5 to 3
- internal_energy: float32 [4], replicated, may hold values from -2 to -0.5
- amplitudes: bfloat16 [4, 2048, 2048], P(None, None, 'pair'), may hold values from -0.125 to 0.125
- cfg_map: int32 [4, 8], replicated, may hold values from 0 to 3
- coupling: float32 [4, 8], replicated, may hold values from 0.5 to 2
Outputs:
- residual: bfloat16 [2048, 4, 2048], P('fit', None, 'pair')
The draws below stay inside these ranges and needn't reach their ends.
All inputs are finite; a program needn't handle non-finite values.
Results may differ from the reference program's by a relative error of at most 0.0044.
Values may be sent and summed in bfloat16 or wider, within the bound.
A program may use at most 64 MiB of HBM per device.

```python
import math
import jax
import jax.numpy as jnp
from jax import lax

V = 2048
NAUX = 8000
J = 4
NTERM = 8
NCFG = 4
N_FIT = 32


def place_ends(array, own_key, low, high):
    place = [jax.random.randint(jax.random.fold_in(own_key, axis), (), 0, length) for axis, length in enumerate(array.shape)]
    longest = array.shape.index(max(array.shape))
    beside = place[:longest] + [(place[longest] + 1) % array.shape[longest]] + place[longest + 1:]
    return array.at[tuple(place)].set(low).at[tuple(beside)].set(high)


def with_spikes(array, stream_key, source, target, blocks, factor):
    owner, partner = [(jnp.arange(array.shape[axis_at]) // (array.shape[axis_at] // blocks)).reshape([-1 if axis == axis_at else 1 for axis in range(array.ndim)]) for axis_at in (source, target)]
    chosen = jax.random.permutation(stream_key, blocks)[partner]
    strong = (owner == chosen) | (owner == (partner + blocks // 2) % blocks)
    return jnp.where(strong, factor * array, array)


def level_of(own_key, extent, shards, low, high):
    def one(axis_at, blocks):
        heights = jax.random.uniform(jax.random.fold_in(jax.random.fold_in(own_key, 6), axis_at), (blocks,), jnp.float32, low / len(shards), high / len(shards))
        return jnp.repeat(jnp.exp(heights), extent[axis_at] // blocks).reshape((-1,) + (1,) * (len(extent) - axis_at - 1))

    gain = one(*shards[0])
    for cut in shards[1:]:
        gain = gain * one(*cut)
    return gain


def gaussian(key, extent, width, reach, split=(), dtype=jnp.bfloat16):
    level = level_of(key, extent, split, -0.22, 0.18) if split else 1.0
    entries = jax.random.normal(key, extent, jnp.float32) * width * level
    return jnp.minimum(jnp.maximum(entries, -reach), reach).astype(dtype)


def bell_draw_with(key, shape, spread, limit, split, heavy, dtype=jnp.bfloat16):
    values = spread * jax.random.normal(key, shape, jnp.float32)
    if split:
        values = values * level_of(key, shape, split, -0.22, 0.18)
    return jnp.clip(with_spikes(values, jax.random.fold_in(key, 3), *heavy), -limit, limit).astype(dtype)


def setup_inputs(seed: int = 0) -> dict:
    splits = jax.random.split(jax.random.key(seed), 8)
    left_factors = bell_draw_with(splits[0], (NAUX, V), (NAUX ** -0.25), 0.6328125, ((0, 32),), (0, 1, 32, 2.75))
    right_factors = gaussian(splits[1], (J, NAUX, V), (NAUX ** -0.25), 0.6328125, ((1, 32), (2, 16)))
    virtual_energy = jnp.clip(jnp.exp(jax.random.uniform(splits[2], (V,), jnp.float32, math.log(0.5), math.log(3.0))), 0.5, 3.0)
    internal_energy = jnp.clip(jax.random.uniform(splits[3], (J,), jnp.float32, -2.0, -0.5), -2.0, -0.5)
    amplitudes = gaussian(splits[4], (NCFG, V, V), V ** -0.5, 0.125, ((2, 16),))
    cfg_map = place_ends(jax.random.randint(splits[5], (J, NTERM), 0, NCFG), jax.random.fold_in(splits[5], 1), 0, NCFG - 1).astype(jnp.int32)
    coupling = jnp.clip(jnp.exp(jax.random.uniform(splits[6], (J, NTERM), jnp.float32, math.log(0.5), math.log(2.0))), 0.5, 2.0)
    return {"left_factors": left_factors, "right_factors": right_factors, "virtual_energy": virtual_energy, "internal_energy": internal_energy, "amplitudes": amplitudes, "cfg_map": cfg_map, "coupling": coupling}


def reference(left_factors, right_factors, virtual_energy, internal_energy, amplitudes, cfg_map, coupling):
    block_rows = NAUX // N_FIT
    left = left_factors.astype(jnp.float32).reshape(N_FIT, block_rows, V)
    right = right_factors.astype(jnp.float32).reshape(J, N_FIT, block_rows, V).transpose(1, 0, 2, 3)

    def add_block(total, pieces):
        left_block, right_block = pieces
        partial_value = jnp.einsum("qa,jqc->ajc", left_block, right_block)
        return total + partial_value, None

    kernel, _ = lax.scan(add_block, jnp.zeros((V, J, V), jnp.float32), (left, right))
    denom = virtual_energy[:, None, None] + virtual_energy[None, None, :] - internal_energy[None, :, None]
    trial = (kernel / denom).astype(jnp.bfloat16).astype(jnp.float32)
    coupled = jnp.zeros((V, J, V), jnp.float32)
    for term in range(NTERM):
        selected = jnp.take(amplitudes, cfg_map[:, term].astype(jnp.int32), axis=0).astype(jnp.float32)
        inner = jnp.einsum("ajc,jcb->ajb", trial, selected)
        coupled = coupled + coupling[None, :, term, None] * inner
    return (kernel + coupled).astype(jnp.bfloat16)
```

```python
import functools

import jax
import jax.numpy as jnp
from jax import lax
from jax.experimental import pallas as pl
from jax.experimental.pallas import tpu as pltpu
from jax.sharding import PartitionSpec as P

MESH = pl.DeviceIdType.MESH
NX, NYL, NYH, NZ, NC = 4, 4, 2, 8, 2
NJ, NTERM, NCFG = 4, 8, 4
ROWS, COLS, V, KPAD = 64, 128, 2048, 256
HALF = NZ // 2


def place(x, yh, yl, z, c):
    return (yl * NZ + z, x * (NYH * NC) + yh * NC + c)


def kernel(
    left_ref, right_ref, ve_ref, ie_ref, cfg_ref, cp_ref, amp_hbm, out_ref,
    at, bt, amp, mix, zin, zout, tot, yin, ker, tr,
    amp_sem, zs, zr, ys, yr, hs, hr, xs, xr, cs, cr,
):
    fit, pair = lax.axis_index("fit"), lax.axis_index("pair")
    z, yl = lax.rem(fit, NZ), lax.div(fit, NZ)
    c, yh, x = lax.rem(pair, NC), lax.rem(lax.div(pair, NC), NYH), lax.div(pair, NYH * NC)

    def zdev(k):
        return place(x, yh, yl, lax.rem(z + k + NZ, NZ), c)

    def ydev(k):
        return place(x, yh, lax.rem(yl + k + NYL, NYL), z, c)

    def xdev(k):
        return place(lax.rem(x + k + NX, NX), yh, yl, z, c)

    hdev = place(x, 1 - yh, yl, z, c)
    cdev = place(x, yh, yl, z, 1 - c)

    barrier = pltpu.get_barrier_semaphore()
    partners = [zdev(1), zdev(-1)] + [ydev(k) for k in (1, 2, 3)] + [xdev(k) for k in (1, 2, 3)] + [hdev, cdev]
    for d in partners:
        pl.semaphore_signal(barrier, inc=1, device_id=d, device_id_type=MESH)

    amp_copy = pltpu.make_async_copy(amp_hbm, amp, amp_sem)
    amp_copy.start()

    depth = left_ref.shape[0]
    at[:, :, :, KPAD - 128 :] = jnp.zeros((NYL, NZ, ROWS, 128), jnp.bfloat16)
    bt[:, KPAD - 16 :, :] = jnp.zeros((NJ, 16, COLS), jnp.bfloat16)
    for j in range(NJ):
        bt[j, :depth, :] = right_ref[j]
    for m in range(V // 128):
        piece = left_ref[:, m * 128 : (m + 1) * 128].T
        for s in range(2):
            block = 2 * m + s
            at[block // NZ, block % NZ, :, :depth] = piece[s * ROWS : (s + 1) * ROWS]

    def chunk(owner, j):
        rows = at[:, owner].reshape(NYL * ROWS, KPAD)
        return jnp.dot(rows, bt[j], preferred_element_type=jnp.float32)

    def reach(j, d):
        return HALF if (j + d) % 2 == 0 else HALF - 1

    def owner_at(d, k):
        return lax.rem(z + (k if d == 0 else NZ - k), NZ)

    def zcopy(j, d, h):
        return pltpu.make_async_remote_copy(
            src_ref=zout.at[d, j, h], dst_ref=zin.at[d, j, h],
            send_sem=zs.at[d, j, h], recv_sem=zr.at[d, j, h],
            device_id=zdev(1 if d == 0 else -1), device_id_type=MESH,
        )

    def zsend(j, d, h):
        k = reach(j, d) - h
        value = chunk(owner_at(d, k), j)
        if h > 0:
            zcopy(j, d, h - 1).wait_recv()
            value = value + zin[d, j, h - 1].astype(jnp.float32)
        zout[d, j, h] = value.astype(jnp.bfloat16)
        zcopy(j, d, h).start()

    def ycopy(j, k):
        return pltpu.make_async_remote_copy(
            src_ref=tot.at[j, lax.rem(yl + k, NYL)], dst_ref=yin.at[j, k - 1],
            send_sem=ys.at[j, k - 1], recv_sem=yr.at[j, k - 1],
            device_id=ydev(k), device_id_type=MESH,
        )

    def zlast(j):
        value = chunk(z, j)
        for d in range(2):
            h = reach(j, d) - 1
            zcopy(j, d, h).wait_recv()
            value = value + zin[d, j, h].astype(jnp.float32)
        tot[j] = value.reshape(NYL, ROWS, COLS)
        for k in (1, 2, 3):
            ycopy(j, k).start()

    def slot(px, ph, pc):
        return px * (NYH * NC) + ph * NC + pc

    def tcopy(j, p, send, recv, device):
        return pltpu.make_async_remote_copy(
            src_ref=tr.at[j, p], dst_ref=tr.at[j, p], send_sem=send, recv_sem=recv,
            device_id=device, device_id_type=MESH,
        )

    def hcopy(j):
        return tcopy(j, pair, hs.at[j], hr.at[j], hdev)

    def xcopy(j, far, k):
        return tcopy(j, slot(x, 1 - yh if far else yh, c), xs.at[j, far, k - 1], xr.at[j, far, k - 1], xdev(k))

    def ccopy(j, i):
        if i == 0:
            p = pair
        elif i == 1:
            p = slot(x, 1 - yh, c)
        elif i < 5:
            p = slot(lax.rem(x + NX - (i - 1), NX), yh, c)
        else:
            p = slot(lax.rem(x + NX - (i - 4), NX), 1 - yh, c)
        return tcopy(j, p, cs.at[j, i], cr.at[j, i], cdev)

    row_line = ve_ref[pl.ds(lax.div(fit, 2), 1), :]
    lanes = lax.broadcasted_iota(jnp.int32, (ROWS, 128), 1)
    wanted = lax.broadcasted_iota(jnp.int32, (ROWS, 128), 0) + lax.rem(fit, 2) * ROWS
    row_energy = jnp.sum(jnp.where(lanes == wanted, row_line, 0.0), axis=1, keepdims=True)
    pair_energy = row_energy + ve_ref[pl.ds(pair, 1), :]

    def trial(j):
        value = tot[j, yl]
        for k in (1, 2, 3):
            ycopy(j, k).wait_recv()
            value = value + yin[j, k - 1]
        ker[j] = value
        tr[j, pair] = (value / (pair_energy - ie_ref[j])).astype(jnp.bfloat16)
        hcopy(j).start()
        for k in (1, 2, 3):
            xcopy(j, 0, k).start()
        ccopy(j, 0).start()

    def spread(j):
        hcopy(j).wait_recv()
        for k in (1, 2, 3):
            xcopy(j, 1, k).start()
        ccopy(j, 1).start()
        for k in (1, 2, 3):
            xcopy(j, 0, k).wait_recv()
            ccopy(j, 1 + k).start()

    def swap(j):
        for k in (1, 2, 3):
            xcopy(j, 1, k).wait_recv()
            ccopy(j, 4 + k).start()

    def finish(j):
        for i in range(8):
            ccopy(j, i).wait_recv()
        value = ker[j]
        for q in range(NX * NYH):
            both = jnp.concatenate([tr[j, 2 * q], tr[j, 2 * q + 1]], axis=1)
            value = value + jnp.dot(
                both, mix[j, q * 2 * COLS : (q + 1) * 2 * COLS], preferred_element_type=jnp.float32
            )
        out_ref[j] = value.astype(jnp.bfloat16)

    weight = []
    for j in range(NJ):
        line = []
        for k in range(NCFG):
            total = jnp.float32(0.0)
            for n in range(NTERM):
                total = total + jnp.where(cfg_ref[j, n] == k, cp_ref[j, n], jnp.float32(0.0))
            line.append(total)
        weight.append(line)

    def combine(part):
        rows = slice(part * 256, (part + 1) * 256)
        parts = [amp[k, rows].astype(jnp.float32) for k in range(NCFG)]
        for j in range(NJ):
            value = weight[j][0] * parts[0]
            for k in range(1, NCFG):
                value = value + weight[j][k] * parts[k]
            mix[j, rows] = value.astype(jnp.bfloat16)

    pl.semaphore_wait(barrier, len(partners))
    for j in range(NJ):
        for d in range(2):
            zsend(j, d, 0)
    amp_copy.wait()
    todo = list(range(8))
    for group in ((0, 1), (2, 3)):
        for h in range(1, HALF):
            for j in group:
                for d in range(2):
                    if h < reach(j, d):
                        zsend(j, d, h)
            if todo:
                combine(todo.pop(0))
                combine(todo.pop(0))
            if group == (2, 3):
                if h == 1:
                    trial(0)
                    trial(1)
                elif h == 2:
                    spread(0)
                    spread(1)
                else:
                    swap(0)
                    swap(1)
        for j in group:
            zlast(j)
    while todo:
        combine(todo.pop(0))
    finish(0)
    finish(1)
    for step in (trial, spread, swap, finish):
        for j in (2, 3):
            step(j)

    for j in range(NJ):
        for d in range(2):
            for h in range(reach(j, d)):
                zcopy(j, d, h).wait_send()
        for k in (1, 2, 3):
            ycopy(j, k).wait_send()
            xcopy(j, 0, k).wait_send()
            xcopy(j, 1, k).wait_send()
        hcopy(j).wait_send()
        for i in range(8):
            ccopy(j, i).wait_send()


def shards(left, right, virtual_energy, internal_energy, amplitudes, cfg_map, coupling):
    vmem = pl.BlockSpec(memory_space=pltpu.VMEM)
    smem = pl.BlockSpec(memory_space=pltpu.SMEM)
    dma = pltpu.SemaphoreType.DMA
    out = pl.pallas_call(
        kernel,
        out_shape=jax.ShapeDtypeStruct((NJ, ROWS, COLS), jnp.bfloat16),
        in_specs=[vmem, vmem, vmem, smem, smem, smem, pl.BlockSpec(memory_space=pl.ANY)],
        out_specs=vmem,
        scratch_shapes=[
            pltpu.VMEM((NYL, NZ, ROWS, KPAD), jnp.bfloat16),
            pltpu.VMEM((NJ, KPAD, COLS), jnp.bfloat16),
            pltpu.VMEM((NCFG, V, COLS), jnp.bfloat16),
            pltpu.VMEM((NJ, V, COLS), jnp.bfloat16),
            pltpu.VMEM((2, NJ, HALF, NYL * ROWS, COLS), jnp.bfloat16),
            pltpu.VMEM((2, NJ, HALF, NYL * ROWS, COLS), jnp.bfloat16),
            pltpu.VMEM((NJ, NYL, ROWS, COLS), jnp.float32),
            pltpu.VMEM((NJ, 3, ROWS, COLS), jnp.float32),
            pltpu.VMEM((NJ, ROWS, COLS), jnp.float32),
            pltpu.VMEM((NJ, NX * NYH * NC, ROWS, COLS), jnp.bfloat16),
            dma,
            dma((2, NJ, HALF)),
            dma((2, NJ, HALF)),
            dma((NJ, 3)),
            dma((NJ, 3)),
            dma((NJ,)),
            dma((NJ,)),
            dma((NJ, 2, 3)),
            dma((NJ, 2, 3)),
            dma((NJ, 8)),
            dma((NJ, 8)),
        ],
        compiler_params=pltpu.CompilerParams(
            collective_id=0, has_side_effects=True, vmem_limit_bytes=48 << 20
        ),
        name="exchange",
    )(left, right, virtual_energy.reshape(V // 128, 128), internal_energy, cfg_map, coupling, amplitudes)
    return jnp.transpose(out, (1, 0, 2))


def solution(mesh):
    placed = (P("fit", None), P(None, "fit", "pair"), P(), P(), P(None, None, "pair"), P(), P())
    return jax.shard_map(
        shards, mesh=mesh, in_specs=placed, out_specs=P("fit", None, "pair"), check_vma=False
    )
```

```python
import jax
import jax.numpy as jnp
from jax import lax
from jax.experimental import pallas as pl
from jax.experimental.pallas import tpu as pltpu
from jax.sharding import PartitionSpec as P

MESH = pl.DeviceIdType.MESH
NX, NYL, NYH, NZ, NC = 4, 4, 2, 8, 2
NY = NYL * NYH
NJ, NTERM, NCFG = 4, 8, 4
ROWS, COLS, V, KPAD = 64, 128, 2048, 256
HALF = NZ // 2
GROUPS = ((0, 1), (2, 3))
RING, GATHER = 0, 1
WIDE = 2 * COLS
RELAY = True
ORDER = (
    ('a', 0), ('a', 1), ('b', 0, 0, 0), ('b', 0, 1, 0), ('z', 3, 0, 0), ('z', 3, 1, 0), ('z', 2, 0, 0),
    ('z', 2, 1, 0), ('z', 1, 0, 0), ('z', 1, 1, 0), ('z', 0, 0, 0), ('z', 0, 1, 0), ('b', 1, 0, 0),
    ('b', 1, 1, 0), ('r', 0), ('a', 2), ('z', 3, 0, 1), ('z', 3, 1, 1), ('z', 2, 0, 1), ('z', 2, 1, 1),
    ('z', 1, 0, 1), ('z', 1, 1, 1), ('z', 0, 0, 1), ('z', 0, 1, 1), ('b', 0, 0, 1), ('b', 0, 1, 1),
    ('b', 1, 0, 1), ('b', 1, 1, 1), ('r', 1), ('ax',), ('z', 3, 0, 2), ('z', 3, 1, 2), ('z', 2, 0, 2),
    ('z', 2, 1, 2), ('z', 1, 0, 2), ('z', 1, 1, 2), ('z', 0, 0, 2), ('z', 0, 1, 2), ('b', 0, 0, 2),
    ('b', 0, 1, 2), ('b', 1, 0, 2), ('b', 1, 1, 2), ('r', 2), ('z', 3, 1, 3), ('z', 2, 0, 3), ('z', 1, 1, 3),
    ('z', 0, 0, 3), ('ac',), ('l', 3), ('l', 2), ('l', 1), ('w',), ('l', 0), ('t', 0), ('t', 1), ('s', 0),
    ('s', 1), ('c', 0), ('c', 1), ('f', 0), ('f', 1),
)


def place(x, yh, yl, z, c):
    return (yl * NZ + z, x * (NYH * NC) + yh * NC + c)


def kernel(
    left_hbm, right_hbm, ve_hbm, ie_hbm, cfg_hbm, cp_hbm, amp_hbm, out_ref,
    left_ref, right_ref, ve_ref, ie_ref, cfg_ref, cp_ref, amp, at, bt,
    zin, zout, tot, yin, bin_, ain, csum, cout, cin, ker, tr,
    in_sem, relay, zs, zr, ys, yr, bs, br, as_, ar, axs, axr, acs, acr, ws, wr, hs, hr, xs, xr, cs, cr,
):
    fit, pair = lax.axis_index("fit"), lax.axis_index("pair")
    z, yl = lax.rem(fit, NZ), lax.div(fit, NZ)
    c, yh, x = lax.rem(pair, NC), lax.rem(lax.div(pair, NC), NYH), lax.div(pair, NYH * NC)
    y = yh * NYL + yl

    def zdev(k):
        return place(x, yh, yl, lax.rem(z + k + NZ, NZ), c)

    def ydev(k):
        return place(x, yh, lax.rem(yl + k + NYL, NYL), z, c)

    def around(k):
        other = lax.rem(y + k + NY, NY)
        return place(x, lax.div(other, NYL), lax.rem(other, NYL), z, c)

    def xdev(k):
        return place(lax.rem(x + k + NX, NX), yh, yl, z, c)

    hdev = place(x, 1 - yh, yl, z, c)
    cdev = place(x, yh, yl, z, 1 - c)

    barrier = pltpu.get_barrier_semaphore()
    near = [zdev(1), zdev(-1), around(1), around(-1), xdev(1), xdev(-1)]
    far = [] if RELAY else (
        [zdev(k) for k in range(2, 7)] + [around(k) for k in range(2, 7)] + [xdev(2)]
    )
    for d in near + far + [cdev]:
        pl.semaphore_signal(barrier, inc=1, device_id=d, device_id_type=MESH)

    loads = [
        pltpu.make_async_copy(source, target, in_sem.at[i])
        for i, (source, target) in enumerate(
            [
                (right_hbm, right_ref), (left_hbm, left_ref), (ve_hbm, ve_ref), (ie_hbm, ie_ref),
                (cfg_hbm, cfg_ref), (cp_hbm, cp_ref), (amp_hbm, amp),
            ]
        )
    ]
    for load in loads:
        load.start()

    sent = []

    def start(copy):
        copy.start()
        sent.append(copy)

    def remote(source, target, send, recv, device):
        return pltpu.make_async_remote_copy(
            src_ref=source, dst_ref=target, send_sem=send, recv_sem=recv, device_id=device, device_id_type=MESH
        )

    def greet(r):
        if RELAY:
            for d in near:
                pl.semaphore_signal(relay.at[r], inc=1, device_id=d, device_id_type=MESH)

    def greeted(r):
        if RELAY:
            pl.semaphore_wait(relay.at[r], len(near))
            if r < 2:
                greet(r + 1)

    depth = left_ref.shape[0]
    at[:, :, :, KPAD - 128 :] = jnp.zeros((NYL, NZ, ROWS, 128), jnp.bfloat16)
    bt[:, KPAD - 16 :, :] = jnp.zeros((2, 16, WIDE), jnp.bfloat16)
    loads[0].wait()
    for g, group in enumerate(GROUPS):
        for i, j in enumerate(group):
            bt[g, :depth, i * COLS : (i + 1) * COLS] = right_ref[:, j, :]
    loads[1].wait()
    for m in range(V // 128):
        piece = left_ref[:, m * 128 : (m + 1) * 128].T
        for s in range(2):
            block = 2 * m + s
            at[block // NZ, block % NZ, :, :depth] = piece[s * ROWS : (s + 1) * ROWS]

    def chunk(owner, u):
        return jnp.dot(
            at[lax.rem(yl + u, NYL), owner], bt[RING], preferred_element_type=jnp.float32
        )

    def reach(u, d):
        return HALF if (u + d) % 2 == 0 else HALF - 1

    def owner_at(d, k):
        return lax.rem(z + (k if d == 0 else NZ - k), NZ)

    def zcopy(u, d, h):
        return remote(
            zout.at[d, u, h], zin.at[d, u, h], zs.at[d, u, h], zr.at[d, u, h], zdev(1 if d == 0 else -1)
        )

    def zsend(u, d, h):
        value = chunk(owner_at(d, reach(u, d) - h), u)
        if h > 0:
            zcopy(u, d, h - 1).wait_recv()
            value = value + zin[d, u, h - 1].astype(jnp.float32)
        zout[d, u, h] = value.astype(jnp.bfloat16)
        start(zcopy(u, d, h))

    def ycopy(u):
        return remote(tot.at[u - 1], yin.at[u - 1], ys.at[u - 1], yr.at[u - 1], ydev(u))

    def zlast(u):
        value = chunk(z, u)
        for d in range(2):
            h = reach(u, d) - 1
            zcopy(u, d, h).wait_recv()
            value = value + zin[d, u, h].astype(jnp.float32)
        if u == 0:
            ker[RING] = value
        else:
            tot[u - 1] = value.astype(jnp.bfloat16)
            start(ycopy(u))

    def bcopy(i, d, h):
        part = pl.ds(i * KPAD // 2, KPAD // 2)
        source = bt.at[GATHER, part] if h == 0 else bin_.at[d * 3 + h - 1, part]
        return remote(
            source, bin_.at[d * 3 + h, part], bs.at[d, h, i], br.at[d, h, i], around(1 if d == 0 else -1)
        )

    def bsend(i, d, h):
        if h > 0:
            bcopy(i, d, h - 1).wait_recv()
        start(bcopy(i, d, h))

    def acopy(k):
        step = (1, -1, 2 - 4 * c)[k]
        return remote(
            at.at[lax.rem(yl + step + NYL, NYL), x * NC + c], ain.at[k, x, c], as_.at[k], ar.at[k], around(step)
        )

    def axcopy(k):
        return remote(ain.at[:, x, c], ain.at[:, x, c], axs.at[k - 1], axr.at[k - 1], xdev(k))

    def axsend():
        for k in range(3):
            acopy(k).wait_recv()
        for k in (2, 1, 3):
            start(axcopy(k))

    def accopy():
        return remote(ain.at[:, :, c], ain.at[:, :, c], acs, acr, cdev)

    def acsend():
        for k in (1, 2, 3):
            axcopy(k).wait_recv()
        start(accopy())

    def wcopy(k):
        return remote(cout.at[lax.rem(z + k, NZ)], cin.at[k - 1], ws.at[k - 1], wr.at[k - 1], zdev(k))

    def wsend():
        low, top, mid = 5 * (1 - lax.div(yl + 3, NYL)), 3 - lax.div(yl + 1, NYL), 4 - 3 * lax.div(yl + 2, NYL)
        value = jnp.dot(at[yl].reshape(NZ * ROWS, KPAD), bt[GATHER], preferred_element_type=jnp.float32)
        for i in range(2):
            for d in range(2):
                bcopy(i, d, 2).wait_recv()
        accopy().wait_recv()
        for k, slot_of in enumerate((low, top, mid)):
            value += jnp.dot(ain[k].reshape(NZ * ROWS, KPAD), bin_[slot_of], preferred_element_type=jnp.float32)
        value = value.reshape(NZ, ROWS, WIDE)
        csum[...] = value
        cout[...] = value.astype(jnp.bfloat16)
        for k in (4, 3, 5, 2, 6, 1, 7):
            start(wcopy(k))

    def wjoin():
        value = csum[z]
        for k in (1, 7, 2, 6, 3, 5, 4):
            wcopy(k).wait_recv()
            value = value + cin[k - 1].astype(jnp.float32)
        ker[GATHER] = value

    def yjoin():
        value = ker[RING]
        for k in (1, 2, 3):
            ycopy(k).wait_recv()
            value = value + yin[k - 1].astype(jnp.float32)
        ker[RING] = value

    def hcopy(g):
        mine = tr.at[g, x, yh, c]
        return remote(mine, mine, hs.at[g], hr.at[g], hdev)

    def xcopy(g, other, k):
        mine = tr.at[g, x, 1 - yh if other else yh, c]
        return remote(mine, mine, xs.at[g, other, k - 1], xr.at[g, other, k - 1], xdev(k))

    def ccopy(g, other):
        mine = tr.at[g, :, 1 - yh if other else yh, c]
        return remote(mine, mine, cs.at[g, other], cr.at[g, other], cdev)

    loads[2].wait()
    row_line = ve_ref[pl.ds(lax.div(fit, 2), 1), :]
    lanes = lax.broadcasted_iota(jnp.int32, (ROWS, 128), 1)
    wanted = lax.broadcasted_iota(jnp.int32, (ROWS, 128), 0) + lax.rem(fit, 2) * ROWS
    row_energy = jnp.sum(jnp.where(lanes == wanted, row_line, 0.0), axis=1, keepdims=True)
    pair_energy = row_energy + ve_ref[pl.ds(pair, 1), :]
    for load in loads[3:6]:
        load.wait()
    weight = []
    for j in range(NJ):
        line = []
        for k in range(NCFG):
            total = jnp.float32(0.0)
            for n in range(NTERM):
                total = total + jnp.where(cfg_ref[j, n] == k, cp_ref[j, n], jnp.float32(0.0))
            line.append(total)
        weight.append(line)

    def trial(g):
        (yjoin if g == RING else wjoin)()
        denominator = jnp.concatenate([pair_energy - ie_ref[j] for j in GROUPS[g]], axis=1)
        tr[g, x, yh, c] = (ker[g] / denominator).astype(jnp.bfloat16)
        start(hcopy(g))
        for k in (2, 1, 3):
            start(xcopy(g, 0, k))

    def spread(g):
        hcopy(g).wait_recv()
        for k in (2, 1, 3):
            start(xcopy(g, 1, k))
        for k in (1, 3, 2):
            xcopy(g, 0, k).wait_recv()
        start(ccopy(g, 0))

    def swap(g):
        for k in (1, 3, 2):
            xcopy(g, 1, k).wait_recv()
        start(ccopy(g, 1))

    def finish(g):
        sums = [jnp.zeros((2 * ROWS, WIDE), jnp.float32) for _ in range(NCFG // 2)]
        for other in (0, 1):
            ccopy(g, other).wait_recv()
            for px in range(NX):
                ph = 1 - yh if other else yh
                pieces = [tr[g, px, ph, pc] for pc in range(NC)]
                both = jnp.concatenate(
                    [
                        jnp.concatenate([piece[:, i * COLS : (i + 1) * COLS] for piece in pieces], axis=1)
                        for i in range(2)
                    ],
                    axis=0,
                )
                rows = pl.ds(pl.multiple_of((px * NYH + ph) * WIDE, WIDE), WIDE)
                for k in range(NCFG // 2):
                    pair_of = jnp.concatenate([amp[2 * k, rows], amp[2 * k + 1, rows]], axis=1)
                    sums[k] += jnp.dot(both, pair_of, preferred_element_type=jnp.float32)
        for i, j in enumerate(GROUPS[g]):
            value = ker[g][:, i * COLS : (i + 1) * COLS]
            for k in range(NCFG):
                part = sums[k // 2][i * ROWS : (i + 1) * ROWS, (k % 2) * COLS : (k % 2 + 1) * COLS]
                value = value + weight[j][k] * part
            out_ref[j] = value.astype(jnp.bfloat16)

    pl.semaphore_wait(barrier, len(near + far) + 1)
    greet(0)
    steps = {
        "r": greeted, "z": zsend, "l": zlast, "b": bsend, "a": lambda k: start(acopy(k)), "ax": axsend,
        "ac": acsend, "w": wsend, "t": trial, "s": spread, "c": swap, "f": finish,
    }
    for step in ORDER:
        if step[0] == "f" and loads:
            loads.pop().wait()
            loads.clear()
        steps[step[0]](*step[1:])
    for copy in sent:
        copy.wait_send()


def shards(left, right, virtual_energy, internal_energy, amplitudes, cfg_map, coupling):
    dma = pltpu.SemaphoreType.DMA
    bf16, f32 = jnp.bfloat16, jnp.float32
    out = pl.pallas_call(
        kernel,
        out_shape=pltpu.VMEM((NJ, ROWS, COLS), bf16),
        in_specs=[pl.BlockSpec(memory_space=pl.ANY)] * 7,
        out_specs=pl.BlockSpec(memory_space=pltpu.VMEM),
        scratch_shapes=[
            pltpu.VMEM(left.shape, bf16),
            pltpu.VMEM((left.shape[0], NJ, COLS), bf16),
            pltpu.VMEM((V // 128, 128), f32),
            pltpu.SMEM((NJ,), f32),
            pltpu.SMEM((NJ, NTERM), jnp.int32),
            pltpu.SMEM((NJ, NTERM), f32),
            pltpu.VMEM((NCFG, V, COLS), bf16),
            pltpu.VMEM((NYL, NZ, ROWS, KPAD), bf16),
            pltpu.VMEM((2, KPAD, WIDE), bf16),
            pltpu.VMEM((2, NYL, HALF, ROWS, WIDE), bf16),
            pltpu.VMEM((2, NYL, HALF, ROWS, WIDE), bf16),
            pltpu.VMEM((NYL - 1, ROWS, WIDE), bf16),
            pltpu.VMEM((NYL - 1, ROWS, WIDE), bf16),
            pltpu.VMEM((6, KPAD, WIDE), bf16),
            pltpu.VMEM((3, NX, NC, ROWS, KPAD), bf16),
            pltpu.VMEM((NZ, ROWS, WIDE), f32),
            pltpu.VMEM((NZ, ROWS, WIDE), bf16),
            pltpu.VMEM((NZ - 1, ROWS, WIDE), bf16),
            pltpu.VMEM((2, ROWS, WIDE), f32),
            pltpu.VMEM((2, NX, NYH, NC, ROWS, WIDE), bf16),
            dma((7,)),
            pltpu.SemaphoreType.REGULAR((3,)),
            dma((2, NYL, HALF)),
            dma((2, NYL, HALF)),
            dma((3,)),
            dma((3,)),
            dma((2, 3, 2)),
            dma((2, 3, 2)),
            dma((3,)),
            dma((3,)),
            dma((3,)),
            dma((3,)),
            dma,
            dma,
            dma((NZ - 1,)),
            dma((NZ - 1,)),
            dma((2,)),
            dma((2,)),
            dma((2, 2, 3)),
            dma((2, 2, 3)),
            dma((2, 2)),
            dma((2, 2)),
        ],
        compiler_params=pltpu.CompilerParams(
            collective_id=0, has_side_effects=True, vmem_limit_bytes=56 << 20
        ),
        name="exchange",
    )(left, jnp.transpose(right, (1, 0, 2)), virtual_energy.reshape(V // 128, 128), internal_energy, cfg_map, coupling, amplitudes)
    return jnp.transpose(out, (1, 0, 2))


def solution(mesh):
    placed = (P("fit", None), P(None, "fit", "pair"), P(), P(), P(None, None, "pair"), P(), P())
    return jax.shard_map(
        shards, mesh=mesh, in_specs=placed, out_specs=P("fit", None, "pair"), check_vma=False
    )
```

```python
import jax
import jax.numpy as jnp
from jax import lax
from jax.experimental import pallas as pl
from jax.experimental.pallas import tpu as pltpu
from jax.sharding import PartitionSpec as P

MESH = pl.DeviceIdType.MESH
NX, NYL, NYH, NZ, NC = 4, 4, 2, 8, 2
NY = NYL * NYH
NJ, NTERM, NCFG = 4, 8, 4
ROWS, COLS, V, KPAD = 64, 128, 2048, 256
HALF = NZ // 2
GROUPS = ((0, 1), (2, 3))
RING, GATHER = 0, 1
WIDE = 2 * COLS
RELAY = True
ORDER = (
    ('T',), ('a', 0), ('a', 1), ('b', 0, 0, 0), ('b', 0, 1, 0), ('z', 3, 0, 0), ('z', 3, 1, 0),
    ('z', 2, 0, 0), ('z', 2, 1, 0), ('z', 1, 0, 0), ('z', 1, 1, 0), ('z', 0, 0, 0), ('z', 0, 1, 0),
    ('b', 1, 0, 0), ('b', 1, 1, 0), ('r', 0), ('a', 2), ('ax', 0), ('z', 3, 0, 1), ('z', 3, 1, 1),
    ('z', 2, 0, 1), ('z', 2, 1, 1), ('z', 1, 0, 1), ('z', 1, 1, 1), ('z', 0, 0, 1), ('z', 0, 1, 1),
    ('b', 0, 0, 1), ('b', 0, 1, 1), ('b', 1, 0, 1), ('b', 1, 1, 1), ('r', 1), ('ax', 1), ('z', 3, 0, 2),
    ('z', 3, 1, 2), ('z', 2, 0, 2), ('z', 2, 1, 2), ('z', 1, 0, 2), ('z', 1, 1, 2), ('z', 0, 0, 2),
    ('z', 0, 1, 2), ('ac', 0), ('b', 0, 0, 2), ('b', 0, 1, 2), ('b', 1, 0, 2), ('b', 1, 1, 2), ('r', 2),
    ('z', 3, 1, 3), ('z', 2, 0, 3), ('z', 1, 1, 3), ('z', 0, 0, 3), ('ac', 1), ('w',), ('l', 3), ('l', 2),
    ('l', 1), ('l', 0), ('t', 0), ('t', 1), ('s', 0), ('s', 1), ('f', 0, 0), ('c', 0), ('f', 1, 0), ('c', 1),
    ('f', 0, 1), ('f', 1, 1),
)


def place(x, yh, yl, z, c):
    return (yl * NZ + z, x * (NYH * NC) + yh * NC + c)


def kernel(
    left_hbm, right_hbm, ve_hbm, ie_hbm, cfg_hbm, cp_hbm, amp_hbm, out_ref,
    left_ref, right_ref, ve_ref, ie_ref, cfg_ref, cp_ref, amp, at, bt,
    zin, zout, tot, yin, bin_, ain, csum, cout, cin, ker, tr,
    in_sem, relay, zs, zr, ys, yr, bs, br, as_, ar, axs, axr, acs, acr, ws, wr, hs, hr, xs, xr, cs, cr,
):
    fit, pair = lax.axis_index("fit"), lax.axis_index("pair")
    z, yl = lax.rem(fit, NZ), lax.div(fit, NZ)
    c, yh, x = lax.rem(pair, NC), lax.rem(lax.div(pair, NC), NYH), lax.div(pair, NYH * NC)
    y = yh * NYL + yl

    def zdev(k):
        return place(x, yh, yl, lax.rem(z + k + NZ, NZ), c)

    def ydev(k):
        return place(x, yh, lax.rem(yl + k + NYL, NYL), z, c)

    def around(k):
        other = lax.rem(y + k + NY, NY)
        return place(x, lax.div(other, NYL), lax.rem(other, NYL), z, c)

    def xdev(k):
        return place(lax.rem(x + k + NX, NX), yh, yl, z, c)

    hdev = place(x, 1 - yh, yl, z, c)
    cdev = place(x, yh, yl, z, 1 - c)

    barrier = pltpu.get_barrier_semaphore()
    near = [zdev(1), zdev(-1), around(1), around(-1), xdev(1), xdev(-1)]
    far = [] if RELAY else (
        [zdev(k) for k in range(2, 7)] + [around(k) for k in range(2, 7)] + [xdev(2)]
    )
    for d in near + far + [cdev]:
        pl.semaphore_signal(barrier, inc=1, device_id=d, device_id_type=MESH)

    loads = [
        pltpu.make_async_copy(source, target, in_sem.at[i])
        for i, (source, target) in enumerate(
            [
                (right_hbm, right_ref), (left_hbm, left_ref), (ve_hbm, ve_ref), (ie_hbm, ie_ref),
                (cfg_hbm, cfg_ref), (cp_hbm, cp_ref), (amp_hbm, amp),
            ]
        )
    ]
    for load in loads[:-1]:
        load.start()

    sent = []

    def start(copy):
        copy.start()
        sent.append(copy)

    def remote(source, target, send, recv, device):
        return pltpu.make_async_remote_copy(
            src_ref=source, dst_ref=target, send_sem=send, recv_sem=recv, device_id=device, device_id_type=MESH
        )

    def greet(r):
        if RELAY:
            for d in near:
                pl.semaphore_signal(relay.at[r], inc=1, device_id=d, device_id_type=MESH)

    def greeted(r):
        if RELAY:
            pl.semaphore_wait(relay.at[r], len(near))
            if r < 2:
                greet(r + 1)

    depth = left_ref.shape[0]
    at[:, :, :, KPAD - 128 :] = jnp.zeros((NYL, NZ, ROWS, 128), jnp.bfloat16)
    bt[:, KPAD - 16 :, :] = jnp.zeros((2, 16, WIDE), jnp.bfloat16)
    loads[0].wait()
    for g, group in enumerate(GROUPS):
        for i, j in enumerate(group):
            bt[g, :depth, i * COLS : (i + 1) * COLS] = right_ref[:, j, :]

    def turn():
        loads[1].wait()
        for m in range(V // 128):
            piece = left_ref[:, m * 128 : (m + 1) * 128].T
            for s in range(2):
                block = 2 * m + s
                at[block // NZ, block % NZ, :, :depth] = piece[s * ROWS : (s + 1) * ROWS]
        loads[-1].start()

    def chunk(owner, u):
        return jnp.dot(
            at[lax.rem(yl + u, NYL), owner], bt[RING], preferred_element_type=jnp.float32
        )

    def reach(u, d):
        return HALF if (u + d) % 2 == 0 else HALF - 1

    def owner_at(d, k):
        return lax.rem(z + (k if d == 0 else NZ - k), NZ)

    def zcopy(u, d, h):
        return remote(
            zout.at[d, u, h], zin.at[d, u, h], zs.at[d, u, h], zr.at[d, u, h], zdev(1 if d == 0 else -1)
        )

    def zsend(u, d, h):
        value = chunk(owner_at(d, reach(u, d) - h), u)
        if h > 0:
            zcopy(u, d, h - 1).wait_recv()
            value = value + zin[d, u, h - 1].astype(jnp.float32)
        zout[d, u, h] = value.astype(jnp.bfloat16)
        start(zcopy(u, d, h))

    def ycopy(u):
        return remote(tot.at[u - 1], yin.at[u - 1], ys.at[u - 1], yr.at[u - 1], ydev(u))

    def zlast(u):
        value = chunk(z, u)
        for d in range(2):
            h = reach(u, d) - 1
            zcopy(u, d, h).wait_recv()
            value = value + zin[d, u, h].astype(jnp.float32)
        if u == 0:
            ker[RING] = value
        else:
            tot[u - 1] = value.astype(jnp.bfloat16)
            start(ycopy(u))

    def bcopy(i, d, h):
        part = pl.ds(i * KPAD // 2, KPAD // 2)
        source = bt.at[GATHER, part] if h == 0 else bin_.at[d * 3 + h - 1, part]
        return remote(
            source, bin_.at[d * 3 + h, part], bs.at[d, h, i], br.at[d, h, i], around(1 if d == 0 else -1)
        )

    def bsend(i, d, h):
        if h > 0:
            bcopy(i, d, h - 1).wait_recv()
        start(bcopy(i, d, h))

    def acopy(k):
        step = (1, -1, 2 - 4 * c)[k]
        return remote(
            at.at[lax.rem(yl + step + NYL, NYL), c * NX + x], ain.at[k, c, x], as_.at[k], ar.at[k], around(step)
        )

    batches = ((0, 2), (2, 1))

    def axcopy(part, k):
        some = ain.at[pl.ds(*batches[part]), c, x]
        return remote(some, some, axs.at[part, k - 1], axr.at[part, k - 1], xdev(k))

    def axsend(part):
        first, count = batches[part]
        for k in range(first, first + count):
            acopy(k).wait_recv()
        for k in (2, 1, 3):
            start(axcopy(part, k))

    def accopy(part):
        some = ain.at[pl.ds(*batches[part]), c]
        return remote(some, some, acs.at[part], acr.at[part], cdev)

    def acsend(part):
        for k in (1, 3, 2):
            axcopy(part, k).wait_recv()
        start(accopy(part))

    def wcopy(owner):
        slot_of = lax.rem(owner + NZ - 1 - z, NZ)
        return remote(
            cout.at[owner], cin.at[slot_of], ws.at[slot_of], wr.at[slot_of], place(x, yh, yl, owner, c)
        )

    def wsend():
        low, top, mid = 5 * (1 - lax.div(yl + 3, NYL)), 3 - lax.div(yl + 1, NYL), 4 - 3 * lax.div(yl + 2, NYL)
        for i in range(2):
            for d in range(2):
                bcopy(i, d, 2).wait_recv()
        for part in range(2):
            accopy(part).wait_recv()
        columns = [bt[GATHER]] + [bin_[slot_of] for slot_of in (low, top, mid)]
        for part in range(2):
            rows = [at[yl, part * HALF : (part + 1) * HALF]] + [ain[s, part] for s in range(3)]
            value = sum(
                jnp.dot(a.reshape(HALF * ROWS, KPAD), b, preferred_element_type=jnp.float32)
                for a, b in zip(rows, columns)
            ).reshape(HALF, ROWS, WIDE)
            csum[part * HALF : (part + 1) * HALF] = value
            cout[part * HALF : (part + 1) * HALF] = value.astype(jnp.bfloat16)
            for owner in range(part * HALF, (part + 1) * HALF):

                @pl.when(z != owner)
                def _():
                    wcopy(owner).start()

    def wdone():
        for owner in range(NZ):

            @pl.when(z != owner)
            def _():
                wcopy(owner).wait_send()

    def wjoin():
        value = csum[z]
        for k in (1, 7, 2, 6, 3, 5, 4):
            remote(cout.at[0], cin.at[k - 1], ws.at[k - 1], wr.at[k - 1], zdev(-k)).wait_recv()
            value = value + cin[k - 1].astype(jnp.float32)
        ker[GATHER] = value

    def yjoin():
        value = ker[RING]
        for k in (1, 2, 3):
            ycopy(k).wait_recv()
            value = value + yin[k - 1].astype(jnp.float32)
        ker[RING] = value

    def hcopy(g):
        mine = tr.at[g, yh, c, x]
        return remote(mine, mine, hs.at[g], hr.at[g], hdev)

    def xcopy(g, other, k):
        mine = tr.at[g, 1 - yh if other else yh, c, x]
        return remote(mine, mine, xs.at[g, other, k - 1], xr.at[g, other, k - 1], xdev(k))

    def ccopy(g, other):
        mine = tr.at[g, 1 - yh if other else yh, c]
        return remote(mine, mine, cs.at[g, other], cr.at[g, other], cdev)

    loads[2].wait()
    row_line = ve_ref[pl.ds(lax.div(fit, 2), 1), :]
    lanes = lax.broadcasted_iota(jnp.int32, (ROWS, 128), 1)
    wanted = lax.broadcasted_iota(jnp.int32, (ROWS, 128), 0) + lax.rem(fit, 2) * ROWS
    row_energy = jnp.sum(jnp.where(lanes == wanted, row_line, 0.0), axis=1, keepdims=True)
    pair_energy = row_energy + ve_ref[pl.ds(pair, 1), :]
    for load in loads[3:6]:
        load.wait()
    weight = []
    for j in range(NJ):
        line = []
        for k in range(NCFG):
            total = jnp.float32(0.0)
            for n in range(NTERM):
                total = total + jnp.where(cfg_ref[j, n] == k, cp_ref[j, n], jnp.float32(0.0))
            line.append(total)
        weight.append(line)

    def trial(g):
        (yjoin if g == RING else wjoin)()
        denominator = jnp.concatenate([pair_energy - ie_ref[j] for j in GROUPS[g]], axis=1)
        tr[g, yh, c, x] = (ker[g] / denominator).astype(jnp.bfloat16)
        start(hcopy(g))
        for k in (2, 1, 3):
            start(xcopy(g, 0, k))

    def spread(g):
        hcopy(g).wait_recv()
        for k in (2, 1, 3):
            start(xcopy(g, 1, k))
        for k in (1, 3, 2):
            xcopy(g, 0, k).wait_recv()
        start(ccopy(g, 0))

    def swap(g):
        for k in (1, 3, 2):
            xcopy(g, 1, k).wait_recv()
        start(ccopy(g, 1))

    def products(g, other):
        ccopy(g, other).wait_recv()
        sums = [jnp.zeros((2 * ROWS, WIDE), jnp.float32) for _ in range(NCFG // 2)]
        ph = 1 - yh if other else yh
        for px in range(NX):
            pieces = [tr[g, ph, pc, px] for pc in range(NC)]
            both = jnp.concatenate(
                [
                    jnp.concatenate([piece[:, i * COLS : (i + 1) * COLS] for piece in pieces], axis=1)
                    for i in range(2)
                ],
                axis=0,
            )
            rows = pl.ds(pl.multiple_of((px * NYH + ph) * WIDE, WIDE), WIDE)
            for k in range(NCFG // 2):
                pair_of = jnp.concatenate([amp[2 * k, rows], amp[2 * k + 1, rows]], axis=1)
                sums[k] += jnp.dot(both, pair_of, preferred_element_type=jnp.float32)
        for i, j in enumerate(GROUPS[g]):
            cols = slice(i * COLS, (i + 1) * COLS)
            value = ker[g][:, cols]
            for k in range(NCFG):
                part = sums[k // 2][i * ROWS : (i + 1) * ROWS, (k % 2) * COLS : (k % 2 + 1) * COLS]
                value = value + weight[j][k] * part
            if other:
                out_ref[j] = value.astype(jnp.bfloat16)
            else:
                ker[g, :, cols] = value

    pl.semaphore_wait(barrier, len(near + far) + 1)
    greet(0)
    steps = {
        "r": greeted, "z": zsend, "l": zlast, "b": bsend, "a": lambda k: start(acopy(k)), "ax": axsend,
        "ac": acsend, "w": wsend, "t": trial, "s": spread, "c": swap, "f": products, "T": turn,
    }
    for step in ORDER:
        if step[0] == "f" and loads:
            loads.pop().wait()
            loads.clear()
        steps[step[0]](*step[1:])
    wdone()
    for copy in sent:
        copy.wait_send()


def shards(left, right, virtual_energy, internal_energy, amplitudes, cfg_map, coupling):
    dma = pltpu.SemaphoreType.DMA
    bf16, f32 = jnp.bfloat16, jnp.float32
    out = pl.pallas_call(
        kernel,
        out_shape=pltpu.VMEM((NJ, ROWS, COLS), bf16),
        in_specs=[pl.BlockSpec(memory_space=pl.ANY)] * 7,
        out_specs=pl.BlockSpec(memory_space=pltpu.VMEM),
        scratch_shapes=[
            pltpu.VMEM(left.shape, bf16),
            pltpu.VMEM((left.shape[0], NJ, COLS), bf16),
            pltpu.VMEM((V // 128, 128), f32),
            pltpu.SMEM((NJ,), f32),
            pltpu.SMEM((NJ, NTERM), jnp.int32),
            pltpu.SMEM((NJ, NTERM), f32),
            pltpu.VMEM((NCFG, V, COLS), bf16),
            pltpu.VMEM((NYL, NZ, ROWS, KPAD), bf16),
            pltpu.VMEM((2, KPAD, WIDE), bf16),
            pltpu.VMEM((2, NYL, HALF, ROWS, WIDE), bf16),
            pltpu.VMEM((2, NYL, HALF, ROWS, WIDE), bf16),
            pltpu.VMEM((NYL - 1, ROWS, WIDE), bf16),
            pltpu.VMEM((NYL - 1, ROWS, WIDE), bf16),
            pltpu.VMEM((6, KPAD, WIDE), bf16),
            pltpu.VMEM((3, NC, NX, ROWS, KPAD), bf16),
            pltpu.VMEM((NZ, ROWS, WIDE), f32),
            pltpu.VMEM((NZ, ROWS, WIDE), bf16),
            pltpu.VMEM((NZ, ROWS, WIDE), bf16),
            pltpu.VMEM((2, ROWS, WIDE), f32),
            pltpu.VMEM((2, NYH, NC, NX, ROWS, WIDE), bf16),
            dma((7,)),
            pltpu.SemaphoreType.REGULAR((3,)),
            dma((2, NYL, HALF)),
            dma((2, NYL, HALF)),
            dma((3,)),
            dma((3,)),
            dma((2, 3, 2)),
            dma((2, 3, 2)),
            dma((3,)),
            dma((3,)),
            dma((2, 3)),
            dma((2, 3)),
            dma((2,)),
            dma((2,)),
            dma((NZ,)),
            dma((NZ,)),
            dma((2,)),
            dma((2,)),
            dma((2, 2, 3)),
            dma((2, 2, 3)),
            dma((2, 2)),
            dma((2, 2)),
        ],
        compiler_params=pltpu.CompilerParams(
            collective_id=0, has_side_effects=True, vmem_limit_bytes=56 << 20
        ),
        name="exchange",
    )(left, jnp.transpose(right, (1, 0, 2)), virtual_energy.reshape(V // 128, 128), internal_energy, cfg_map, coupling, amplitudes)
    return jnp.transpose(out, (1, 0, 2))


def solution(mesh):
    placed = (P("fit", None), P(None, "fit", "pair"), P(), P(), P(None, None, "pair"), P(), P())
    return jax.shard_map(
        shards, mesh=mesh, in_specs=placed, out_specs=P("fit", None, "pair"), check_vma=False
    )
```

```python
import jax
import jax.numpy as jnp
from jax import lax
from jax.experimental import pallas as pl
from jax.experimental.pallas import tpu as pltpu
from jax.sharding import PartitionSpec as P

MESH = pl.DeviceIdType.MESH
NX, NYL, NYH, NZ, NC = 4, 4, 2, 8, 2
NY = NYL * NYH
NJ, NTERM, NCFG = 4, 8, 4
ROWS, COLS, V, KPAD = 64, 128, 2048, 256
HALF = NZ // 2
GROUPS = ((0, 1), (2, 3))
RING, GATHER = 0, 1
WIDE = 2 * COLS
RELAY = True
ORDER = (
    ('T',), ('a', 0), ('a', 1), ('b', 0, 0, 0), ('b', 0, 1, 0), ('p', 4), ('p', 3), ('p', 5), ('z', 3, 0, 0),
    ('z', 3, 1, 0), ('z', 2, 0, 0), ('z', 2, 1, 0), ('z', 1, 0, 0), ('z', 1, 1, 0), ('z', 0, 0, 0),
    ('z', 0, 1, 0), ('b', 1, 0, 0), ('b', 1, 1, 0), ('r', 0), ('a', 2), ('p', 2), ('p', 6), ('p', 1),
    ('p', 7), ('p', 0), ('ax', 0), ('z', 3, 0, 1), ('z', 3, 1, 1), ('z', 2, 0, 1), ('z', 2, 1, 1),
    ('z', 1, 0, 1), ('z', 1, 1, 1), ('z', 0, 0, 1), ('z', 0, 1, 1), ('b', 0, 0, 1), ('b', 0, 1, 1),
    ('b', 1, 0, 1), ('b', 1, 1, 1), ('r', 1), ('ax', 1), ('z', 3, 0, 2), ('z', 3, 1, 2), ('z', 2, 0, 2),
    ('z', 2, 1, 2), ('z', 1, 0, 2), ('z', 1, 1, 2), ('z', 0, 0, 2), ('z', 0, 1, 2), ('ac', 0), ('b', 0, 0, 2),
    ('b', 0, 1, 2), ('b', 1, 0, 2), ('b', 1, 1, 2), ('r', 2), ('z', 3, 1, 3), ('z', 2, 0, 3), ('z', 1, 1, 3),
    ('z', 0, 0, 3), ('ac', 1), ('l', 3), ('w',), ('l', 2), ('l', 1), ('l', 0), ('t', 0), ('t', 1), ('wd',),
    ('d',), ('s', 0), ('s', 1), ('f', 0, 0), ('c', 0), ('f', 1, 0), ('c', 1), ('d',), ('f', 0, 1),
    ('f', 1, 1),
)


def place(x, yh, yl, z, c):
    return (yl * NZ + z, x * (NYH * NC) + yh * NC + c)


def kernel(
    left_hbm, right_hbm, ve_hbm, ie_hbm, cfg_hbm, cp_hbm, amp_hbm, out_ref,
    left_ref, right_ref, ve_ref, ie_ref, cfg_ref, cp_ref, amp, at, bt,
    pre, zin, zout, tot, yin, bin_, ain, csum, cout, cin, ker, tr,
    in_sem, relay, zs, zr, ys, yr, bs, br, as_, ar, axs, axr, acs, acr, ws, wr, hs, hr, xs, xr, cs, cr,
):
    fit, pair = lax.axis_index("fit"), lax.axis_index("pair")
    z, yl = lax.rem(fit, NZ), lax.div(fit, NZ)
    c, yh, x = lax.rem(pair, NC), lax.rem(lax.div(pair, NC), NYH), lax.div(pair, NYH * NC)
    y = yh * NYL + yl

    def zdev(k):
        return place(x, yh, yl, lax.rem(z + k + NZ, NZ), c)

    def ydev(k):
        return place(x, yh, lax.rem(yl + k + NYL, NYL), z, c)

    def around(k):
        other = lax.rem(y + k + NY, NY)
        return place(x, lax.div(other, NYL), lax.rem(other, NYL), z, c)

    def xdev(k):
        return place(lax.rem(x + k + NX, NX), yh, yl, z, c)

    hdev = place(x, 1 - yh, yl, z, c)
    cdev = place(x, yh, yl, z, 1 - c)

    barrier = pltpu.get_barrier_semaphore()
    near = [zdev(1), zdev(-1), around(1), around(-1), xdev(1), xdev(-1)]
    far = [] if RELAY else (
        [zdev(k) for k in range(2, 7)] + [around(k) for k in range(2, 7)] + [xdev(2)]
    )
    for d in near + far + [cdev]:
        pl.semaphore_signal(barrier, inc=1, device_id=d, device_id_type=MESH)

    loads = [
        pltpu.make_async_copy(source, target, in_sem.at[i])
        for i, (source, target) in enumerate(
            [
                (right_hbm, right_ref), (left_hbm, left_ref), (ve_hbm, ve_ref), (ie_hbm, ie_ref),
                (cfg_hbm, cfg_ref), (cp_hbm, cp_ref), (amp_hbm, amp),
            ]
        )
    ]
    for load in loads[:-1]:
        load.start()

    sent = []

    def start(copy):
        copy.start()
        sent.append(copy)

    def remote(source, target, send, recv, device):
        return pltpu.make_async_remote_copy(
            src_ref=source, dst_ref=target, send_sem=send, recv_sem=recv, device_id=device, device_id_type=MESH
        )

    def greet(r):
        if RELAY:
            for d in near:
                pl.semaphore_signal(relay.at[r], inc=1, device_id=d, device_id_type=MESH)

    def greeted(r):
        if RELAY:
            pl.semaphore_wait(relay.at[r], len(near))
            if r < 2:
                greet(r + 1)

    depth = left_ref.shape[0]
    at[:, :, :, KPAD - 128 :] = jnp.zeros((NYL, NZ, ROWS, 128), jnp.bfloat16)
    bt[:, KPAD - 16 :, :] = jnp.zeros((2, 16, WIDE), jnp.bfloat16)
    loads[0].wait()
    for g, group in enumerate(GROUPS):
        for i, j in enumerate(group):
            bt[g, :depth, i * COLS : (i + 1) * COLS] = right_ref[:, j, :]

    def turn():
        loads[1].wait()
        for m in range(V // 128):
            piece = left_ref[:, m * 128 : (m + 1) * 128].T
            for s in range(2):
                block = 2 * m + s
                at[block // NZ, block % NZ, :, :depth] = piece[s * ROWS : (s + 1) * ROWS]
        loads[-1].start()

    def prepare(k):
        owner = lax.rem(z + k, NZ)
        rows = at[:, owner].reshape(NYL * ROWS, KPAD)
        value = jnp.dot(rows, bt[RING], preferred_element_type=jnp.float32)
        pre[owner] = value.reshape(NYL, ROWS, WIDE)

    def chunk(owner, u):
        return pre[owner, lax.rem(yl + u, NYL)]

    def reach(u, d):
        return HALF if (u + d) % 2 == 0 else HALF - 1

    def owner_at(d, k):
        return lax.rem(z + (k if d == 0 else NZ - k), NZ)

    def zcopy(u, d, h):
        return remote(
            zout.at[d, u, h], zin.at[d, u, h], zs.at[d, u, h], zr.at[d, u, h], zdev(1 if d == 0 else -1)
        )

    def zsend(u, d, h):
        value = chunk(owner_at(d, reach(u, d) - h), u)
        if h > 0:
            zcopy(u, d, h - 1).wait_recv()
            value = value + zin[d, u, h - 1].astype(jnp.float32)
        zout[d, u, h] = value.astype(jnp.bfloat16)
        start(zcopy(u, d, h))

    def ycopy(u):
        return remote(tot.at[u - 1], yin.at[u - 1], ys.at[u - 1], yr.at[u - 1], ydev(u))

    def zlast(u):
        value = chunk(z, u)
        for d in range(2):
            h = reach(u, d) - 1
            zcopy(u, d, h).wait_recv()
            value = value + zin[d, u, h].astype(jnp.float32)
        if u == 0:
            ker[RING] = value
        else:
            tot[u - 1] = value.astype(jnp.bfloat16)
            start(ycopy(u))

    def bcopy(i, d, h):
        part = pl.ds(i * KPAD // 2, KPAD // 2)
        source = bt.at[GATHER, part] if h == 0 else bin_.at[d * 3 + h - 1, part]
        return remote(
            source, bin_.at[d * 3 + h, part], bs.at[d, h, i], br.at[d, h, i], around(1 if d == 0 else -1)
        )

    def bsend(i, d, h):
        if h > 0:
            bcopy(i, d, h - 1).wait_recv()
        start(bcopy(i, d, h))

    def acopy(k):
        step = (1, -1, 2 - 4 * c)[k]
        return remote(
            at.at[lax.rem(yl + step + NYL, NYL), c * NX + x], ain.at[k, c, x], as_.at[k], ar.at[k], around(step)
        )

    batches = ((0, 2), (2, 1))

    def axcopy(part, k):
        some = ain.at[pl.ds(*batches[part]), c, x]
        return remote(some, some, axs.at[part, k - 1], axr.at[part, k - 1], xdev(k))

    def axsend(part):
        first, count = batches[part]
        for k in range(first, first + count):
            acopy(k).wait_recv()
        for k in (2, 1, 3):
            start(axcopy(part, k))

    def accopy(part):
        some = ain.at[pl.ds(*batches[part]), c]
        return remote(some, some, acs.at[part], acr.at[part], cdev)

    def acsend(part):
        for k in (1, 3, 2):
            axcopy(part, k).wait_recv()
        start(accopy(part))

    def wcopy(owner):
        slot_of = lax.rem(owner + NZ - 1 - z, NZ)
        return remote(
            cout.at[owner], cin.at[slot_of], ws.at[slot_of], wr.at[slot_of], place(x, yh, yl, owner, c)
        )

    def wsend():
        low, top, mid = 5 * (1 - lax.div(yl + 3, NYL)), 3 - lax.div(yl + 1, NYL), 4 - 3 * lax.div(yl + 2, NYL)
        for i in range(2):
            for d in range(2):
                bcopy(i, d, 2).wait_recv()
        for part in range(2):
            accopy(part).wait_recv()
        columns = [bt[GATHER]] + [bin_[slot_of] for slot_of in (low, top, mid)]
        for part in range(2):
            rows = [at[yl, part * HALF : (part + 1) * HALF]] + [ain[s, part] for s in range(3)]
            value = sum(
                jnp.dot(a.reshape(HALF * ROWS, KPAD), b, preferred_element_type=jnp.float32)
                for a, b in zip(rows, columns)
            ).reshape(HALF, ROWS, WIDE)
            csum[part * HALF : (part + 1) * HALF] = value
            cout[part * HALF : (part + 1) * HALF] = value.astype(jnp.bfloat16)
            for owner in range(part * HALF, (part + 1) * HALF):

                @pl.when(z != owner)
                def _():
                    wcopy(owner).start()

    def wdone():
        for owner in range(NZ):

            @pl.when(z != owner)
            def _():
                wcopy(owner).wait_send()

    def wjoin():
        value = csum[z]
        for k in (1, 7, 2, 6, 3, 5, 4):
            remote(cout.at[0], cin.at[k - 1], ws.at[k - 1], wr.at[k - 1], zdev(-k)).wait_recv()
            value = value + cin[k - 1].astype(jnp.float32)
        ker[GATHER] = value

    def yjoin():
        value = ker[RING]
        for k in (1, 2, 3):
            ycopy(k).wait_recv()
            value = value + yin[k - 1].astype(jnp.float32)
        ker[RING] = value

    def hcopy(g):
        mine = tr.at[g, yh, c, x]
        return remote(mine, mine, hs.at[g], hr.at[g], hdev)

    def xcopy(g, other, k):
        mine = tr.at[g, 1 - yh if other else yh, c, x]
        return remote(mine, mine, xs.at[g, other, k - 1], xr.at[g, other, k - 1], xdev(k))

    def ccopy(g, other):
        mine = tr.at[g, 1 - yh if other else yh, c]
        return remote(mine, mine, cs.at[g, other], cr.at[g, other], cdev)

    loads[2].wait()
    row_line = ve_ref[pl.ds(lax.div(fit, 2), 1), :]
    lanes = lax.broadcasted_iota(jnp.int32, (ROWS, 128), 1)
    wanted = lax.broadcasted_iota(jnp.int32, (ROWS, 128), 0) + lax.rem(fit, 2) * ROWS
    row_energy = jnp.sum(jnp.where(lanes == wanted, row_line, 0.0), axis=1, keepdims=True)
    pair_energy = row_energy + ve_ref[pl.ds(pair, 1), :]
    for load in loads[3:6]:
        load.wait()
    weight = []
    for j in range(NJ):
        line = []
        for k in range(NCFG):
            total = jnp.float32(0.0)
            for n in range(NTERM):
                total = total + jnp.where(cfg_ref[j, n] == k, cp_ref[j, n], jnp.float32(0.0))
            line.append(total)
        weight.append(line)

    def trial(g):
        (yjoin if g == RING else wjoin)()
        denominator = jnp.concatenate([pair_energy - ie_ref[j] for j in GROUPS[g]], axis=1)
        tr[g, yh, c, x] = (ker[g] / denominator).astype(jnp.bfloat16)
        start(hcopy(g))
        for k in (2, 1, 3):
            start(xcopy(g, 0, k))

    def spread(g):
        hcopy(g).wait_recv()
        for k in (2, 1, 3):
            start(xcopy(g, 1, k))
        for k in (1, 3, 2):
            xcopy(g, 0, k).wait_recv()
        start(ccopy(g, 0))

    def swap(g):
        for k in (1, 3, 2):
            xcopy(g, 1, k).wait_recv()
        start(ccopy(g, 1))

    def products(g, other):
        ccopy(g, other).wait_recv()
        sums = [jnp.zeros((2 * ROWS, WIDE), jnp.float32) for _ in range(NCFG // 2)]
        ph = 1 - yh if other else yh
        for px in range(NX):
            pieces = [tr[g, ph, pc, px] for pc in range(NC)]
            both = jnp.concatenate(
                [
                    jnp.concatenate([piece[:, i * COLS : (i + 1) * COLS] for piece in pieces], axis=1)
                    for i in range(2)
                ],
                axis=0,
            )
            rows = pl.ds(pl.multiple_of((px * NYH + ph) * WIDE, WIDE), WIDE)
            for k in range(NCFG // 2):
                pair_of = jnp.concatenate([amp[2 * k, rows], amp[2 * k + 1, rows]], axis=1)
                sums[k] += jnp.dot(both, pair_of, preferred_element_type=jnp.float32)
        for i, j in enumerate(GROUPS[g]):
            cols = slice(i * COLS, (i + 1) * COLS)
            value = ker[g][:, cols]
            for k in range(NCFG):
                part = sums[k // 2][i * ROWS : (i + 1) * ROWS, (k % 2) * COLS : (k % 2 + 1) * COLS]
                value = value + weight[j][k] * part
            if other:
                out_ref[j] = value.astype(jnp.bfloat16)
            else:
                ker[g, :, cols] = value

    pl.semaphore_wait(barrier, len(near + far) + 1)
    greet(0)
    def drain():
        for copy in sent:
            copy.wait_send()
        sent.clear()

    steps = {
        "r": greeted, "z": zsend, "l": zlast, "b": bsend, "a": lambda k: start(acopy(k)), "ax": axsend,
        "ac": acsend, "w": wsend, "t": trial, "s": spread, "c": swap, "f": products, "T": turn, "p": prepare, "d": drain, "wd": wdone,
    }
    for step in ORDER:
        if step[0] == "f" and loads:
            loads.pop().wait()
            loads.clear()
        steps[step[0]](*step[1:])
    drain()


def shards(left, right, virtual_energy, internal_energy, amplitudes, cfg_map, coupling):
    dma = pltpu.SemaphoreType.DMA
    bf16, f32 = jnp.bfloat16, jnp.float32
    out = pl.pallas_call(
        kernel,
        out_shape=pltpu.VMEM((NJ, ROWS, COLS), bf16),
        in_specs=[pl.BlockSpec(memory_space=pl.ANY)] * 7,
        out_specs=pl.BlockSpec(memory_space=pltpu.VMEM),
        scratch_shapes=[
            pltpu.VMEM(left.shape, bf16),
            pltpu.VMEM((left.shape[0], NJ, COLS), bf16),
            pltpu.VMEM((V // 128, 128), f32),
            pltpu.SMEM((NJ,), f32),
            pltpu.SMEM((NJ, NTERM), jnp.int32),
            pltpu.SMEM((NJ, NTERM), f32),
            pltpu.VMEM((NCFG, V, COLS), bf16),
            pltpu.VMEM((NYL, NZ, ROWS, KPAD), bf16),
            pltpu.VMEM((2, KPAD, WIDE), bf16),
            pltpu.VMEM((NZ, NYL, ROWS, WIDE), f32),
            pltpu.VMEM((2, NYL, HALF, ROWS, WIDE), bf16),
            pltpu.VMEM((2, NYL, HALF, ROWS, WIDE), bf16),
            pltpu.VMEM((NYL - 1, ROWS, WIDE), bf16),
            pltpu.VMEM((NYL - 1, ROWS, WIDE), bf16),
            pltpu.VMEM((6, KPAD, WIDE), bf16),
            pltpu.VMEM((3, NC, NX, ROWS, KPAD), bf16),
            pltpu.VMEM((NZ, ROWS, WIDE), f32),
            pltpu.VMEM((NZ, ROWS, WIDE), bf16),
            pltpu.VMEM((NZ, ROWS, WIDE), bf16),
            pltpu.VMEM((2, ROWS, WIDE), f32),
            pltpu.VMEM((2, NYH, NC, NX, ROWS, WIDE), bf16),
            dma((7,)),
            pltpu.SemaphoreType.REGULAR((3,)),
            dma((2, NYL, HALF)),
            dma((2, NYL, HALF)),
            dma((3,)),
            dma((3,)),
            dma((2, 3, 2)),
            dma((2, 3, 2)),
            dma((3,)),
            dma((3,)),
            dma((2, 3)),
            dma((2, 3)),
            dma((2,)),
            dma((2,)),
            dma((NZ,)),
            dma((NZ,)),
            dma((2,)),
            dma((2,)),
            dma((2, 2, 3)),
            dma((2, 2, 3)),
            dma((2, 2)),
            dma((2, 2)),
        ],
        compiler_params=pltpu.CompilerParams(
            collective_id=0, has_side_effects=True, vmem_limit_bytes=56 << 20
        ),
        name="exchange",
    )(left, jnp.transpose(right, (1, 0, 2)), virtual_energy.reshape(V // 128, 128), internal_energy, cfg_map, coupling, amplitudes)
    return jnp.transpose(out, (1, 0, 2))


def solution(mesh):
    placed = (P("fit", None), P(None, "fit", "pair"), P(), P(), P(None, None, "pair"), P(), P())
    return jax.shard_map(
        shards, mesh=mesh, in_specs=placed, out_specs=P("fit", None, "pair"), check_vma=False
    )
```

```python
import jax
import jax.numpy as jnp
from jax import lax
from jax.experimental import pallas as pl
from jax.experimental.pallas import tpu as pltpu
from jax.sharding import PartitionSpec as P

MESH = pl.DeviceIdType.MESH
NX, NYL, NYH, NZ, NC = 4, 4, 2, 8, 2
NY = NYL * NYH
NJ, NTERM, NCFG = 4, 8, 4
ROWS, COLS, V, KPAD = 64, 128, 2048, 256
HALF = NZ // 2
GROUPS = ((0, 1), (2, 3))
RING, GATHER = 0, 1
WIDE = 2 * COLS
RELAY = True
ORDER = (
    ('T',), ('a', 0), ('a', 1), ('b', 0, 0, 0), ('b', 0, 1, 0), ('p', 4), ('p', 3), ('p', 5), ('z', 3, 0, 0),
    ('z', 3, 1, 0), ('z', 2, 0, 0), ('z', 2, 1, 0), ('z', 1, 0, 0), ('z', 1, 1, 0), ('z', 0, 0, 0),
    ('z', 0, 1, 0), ('b', 1, 0, 0), ('b', 1, 1, 0), ('r', 0), ('a', 2), ('p', 2), ('p', 6), ('p', 1),
    ('p', 7), ('p', 0), ('ax', 0), ('z', 3, 0, 1), ('z', 3, 1, 1), ('z', 2, 0, 1), ('z', 2, 1, 1),
    ('z', 1, 0, 1), ('z', 1, 1, 1), ('z', 0, 0, 1), ('z', 0, 1, 1), ('b', 0, 0, 1), ('b', 0, 1, 1),
    ('b', 1, 0, 1), ('b', 1, 1, 1), ('m',), ('r', 1), ('ax', 1), ('z', 3, 0, 2), ('z', 3, 1, 2),
    ('z', 2, 0, 2), ('z', 2, 1, 2), ('z', 1, 0, 2), ('z', 1, 1, 2), ('z', 0, 0, 2), ('z', 0, 1, 2), ('ac', 0),
    ('b', 0, 0, 2), ('b', 0, 1, 2), ('b', 1, 0, 2), ('b', 1, 1, 2), ('r', 2), ('z', 3, 1, 3), ('z', 2, 0, 3),
    ('z', 1, 1, 3), ('z', 0, 0, 3), ('ac', 1), ('l', 3), ('w',), ('l', 2), ('l', 1), ('l', 0), ('t', 0),
    ('t', 1), ('wd',), ('d',), ('s', 0), ('s', 1), ('f', 0, 0), ('c', 0), ('f', 1, 0), ('c', 1), ('d',),
    ('f', 0, 1), ('f', 1, 1),
)


def place(x, yh, yl, z, c):
    return (yl * NZ + z, x * (NYH * NC) + yh * NC + c)


def kernel(
    left_hbm, right_hbm, ve_hbm, ie_hbm, cfg_hbm, cp_hbm, amp_hbm, out_ref,
    left_ref, right_ref, ve_ref, ie_ref, cfg_ref, cp_ref, amp, at, bt,
    pre, zin, zout, tot, yin, bin_, ain, csum, cout, cin, ker, tr,
    in_sem, relay, zs, zr, ys, yr, bs, br, as_, ar, axs, axr, acs, acr, ws, wr, hs, hr, xs, xr, cs, cr,
):
    fit, pair = lax.axis_index("fit"), lax.axis_index("pair")
    z, yl = lax.rem(fit, NZ), lax.div(fit, NZ)
    c, yh, x = lax.rem(pair, NC), lax.rem(lax.div(pair, NC), NYH), lax.div(pair, NYH * NC)
    y = yh * NYL + yl

    def zdev(k):
        return place(x, yh, yl, lax.rem(z + k + NZ, NZ), c)

    def ydev(k):
        return place(x, yh, lax.rem(yl + k + NYL, NYL), z, c)

    def around(k):
        other = lax.rem(y + k + NY, NY)
        return place(x, lax.div(other, NYL), lax.rem(other, NYL), z, c)

    def xdev(k):
        return place(lax.rem(x + k + NX, NX), yh, yl, z, c)

    hdev = place(x, 1 - yh, yl, z, c)
    cdev = place(x, yh, yl, z, 1 - c)

    barrier = pltpu.get_barrier_semaphore()
    near = [zdev(1), zdev(-1), around(1), around(-1), xdev(1), xdev(-1)]
    far = [] if RELAY else (
        [zdev(k) for k in range(2, 7)] + [around(k) for k in range(2, 7)] + [xdev(2)]
    )
    for d in near + far + [cdev]:
        pl.semaphore_signal(barrier, inc=1, device_id=d, device_id_type=MESH)

    loads = [
        pltpu.make_async_copy(source, target, in_sem.at[i])
        for i, (source, target) in enumerate(
            [
                (right_hbm, right_ref), (left_hbm, left_ref), (ve_hbm, ve_ref), (ie_hbm, ie_ref),
                (cfg_hbm, cfg_ref), (cp_hbm, cp_ref), (amp_hbm, amp),
            ]
        )
    ]
    for load in loads[:-1]:
        load.start()

    sent = []

    def start(copy):
        copy.start()
        sent.append(copy)

    def remote(source, target, send, recv, device):
        return pltpu.make_async_remote_copy(
            src_ref=source, dst_ref=target, send_sem=send, recv_sem=recv, device_id=device, device_id_type=MESH
        )

    def greet(r):
        if RELAY:
            for d in near:
                pl.semaphore_signal(relay.at[r], inc=1, device_id=d, device_id_type=MESH)

    def greeted(r):
        if RELAY:
            pl.semaphore_wait(relay.at[r], len(near))
            if r < 2:
                greet(r + 1)

    depth = left_ref.shape[0]
    at[:, :, :, KPAD - 128 :] = jnp.zeros((NYL, NZ, ROWS, 128), jnp.bfloat16)
    bt[:, KPAD - 16 :, :] = jnp.zeros((2, 16, WIDE), jnp.bfloat16)
    loads[0].wait()
    for g, group in enumerate(GROUPS):
        for i, j in enumerate(group):
            bt[g, :depth, i * COLS : (i + 1) * COLS] = right_ref[:, j, :]

    def turn():
        loads[1].wait()
        for m in range(V // 128):
            piece = left_ref[:, m * 128 : (m + 1) * 128].T
            for s in range(2):
                block = 2 * m + s
                at[block // NZ, block % NZ, :, :depth] = piece[s * ROWS : (s + 1) * ROWS]
        loads[-1].start()

    def prepare(k):
        owner = lax.rem(z + k, NZ)
        rows = at[:, owner].reshape(NYL * ROWS, KPAD)
        value = jnp.dot(rows, bt[RING], preferred_element_type=jnp.float32)
        pre[owner] = value.reshape(NYL, ROWS, WIDE)

    def chunk(owner, u):
        return pre[owner, lax.rem(yl + u, NYL)]

    def reach(u, d):
        return HALF if (u + d) % 2 == 0 else HALF - 1

    def owner_at(d, k):
        return lax.rem(z + (k if d == 0 else NZ - k), NZ)

    def zcopy(u, d, h):
        return remote(
            zout.at[d, u, h], zin.at[d, u, h], zs.at[d, u, h], zr.at[d, u, h], zdev(1 if d == 0 else -1)
        )

    def zsend(u, d, h):
        value = chunk(owner_at(d, reach(u, d) - h), u)
        if h > 0:
            zcopy(u, d, h - 1).wait_recv()
            value = value + zin[d, u, h - 1].astype(jnp.float32)
        zout[d, u, h] = value.astype(jnp.bfloat16)
        start(zcopy(u, d, h))

    def ycopy(u):
        return remote(tot.at[u - 1], yin.at[u - 1], ys.at[u - 1], yr.at[u - 1], ydev(u))

    def zlast(u):
        value = chunk(z, u)
        for d in range(2):
            h = reach(u, d) - 1
            zcopy(u, d, h).wait_recv()
            value = value + zin[d, u, h].astype(jnp.float32)
        if u == 0:
            ker[RING] = value
        else:
            tot[u - 1] = value.astype(jnp.bfloat16)
            start(ycopy(u))

    def bcopy(i, d, h):
        part = pl.ds(i * KPAD // 2, KPAD // 2)
        source = bt.at[GATHER, part] if h == 0 else bin_.at[d * 3 + h - 1, part]
        return remote(
            source, bin_.at[d * 3 + h, part], bs.at[d, h, i], br.at[d, h, i], around(1 if d == 0 else -1)
        )

    def bsend(i, d, h):
        if h > 0:
            bcopy(i, d, h - 1).wait_recv()
        start(bcopy(i, d, h))

    def acopy(k):
        step = (1, -1, 2 - 4 * c)[k]
        return remote(
            at.at[lax.rem(yl + step + NYL, NYL), c * NX + x], ain.at[k, c, x], as_.at[k], ar.at[k], around(step)
        )

    batches = ((0, 2), (2, 1))

    def axcopy(part, k):
        some = ain.at[pl.ds(*batches[part]), c, x]
        return remote(some, some, axs.at[part, k - 1], axr.at[part, k - 1], xdev(k))

    def axsend(part):
        first, count = batches[part]
        for k in range(first, first + count):
            acopy(k).wait_recv()
        for k in (2, 1, 3):
            start(axcopy(part, k))

    def accopy(part):
        some = ain.at[pl.ds(*batches[part]), c]
        return remote(some, some, acs.at[part], acr.at[part], cdev)

    def acsend(part):
        for k in (1, 3, 2):
            axcopy(part, k).wait_recv()
        start(accopy(part))

    def wcopy(owner):
        slot_of = lax.rem(owner + NZ - 1 - z, NZ)
        return remote(
            cout.at[owner], cin.at[slot_of], ws.at[slot_of], wr.at[slot_of], place(x, yh, yl, owner, c)
        )

    def wsend():
        low, top, mid = 5 * (1 - lax.div(yl + 3, NYL)), 3 - lax.div(yl + 1, NYL), 4 - 3 * lax.div(yl + 2, NYL)
        for i in range(2):
            for d in range(2):
                bcopy(i, d, 2).wait_recv()
        for part in range(2):
            accopy(part).wait_recv()
        columns = [bt[GATHER]] + [bin_[slot_of] for slot_of in (low, top, mid)]
        for part in range(2):
            rows = [at[yl, part * HALF : (part + 1) * HALF]] + [ain[s, part] for s in range(3)]
            value = sum(
                jnp.dot(a.reshape(HALF * ROWS, KPAD), b, preferred_element_type=jnp.float32)
                for a, b in zip(rows, columns)
            ).reshape(HALF, ROWS, WIDE)
            csum[part * HALF : (part + 1) * HALF] = value
            cout[part * HALF : (part + 1) * HALF] = value.astype(jnp.bfloat16)
            for owner in range(part * HALF, (part + 1) * HALF):

                @pl.when(z != owner)
                def _():
                    wcopy(owner).start()

    def wdone():
        for owner in range(NZ):

            @pl.when(z != owner)
            def _():
                wcopy(owner).wait_send()

    def wjoin():
        value = csum[z]
        for k in (1, 7, 2, 6, 3, 5, 4):
            remote(cout.at[0], cin.at[k - 1], ws.at[k - 1], wr.at[k - 1], zdev(-k)).wait_recv()
            value = value + cin[k - 1].astype(jnp.float32)
        ker[GATHER] = value

    def yjoin():
        value = ker[RING]
        for k in (1, 2, 3):
            ycopy(k).wait_recv()
            value = value + yin[k - 1].astype(jnp.float32)
        ker[RING] = value

    def hcopy(g):
        mine = tr.at[g, yh, c, x]
        return remote(mine, mine, hs.at[g], hr.at[g], hdev)

    def xcopy(g, other, k):
        mine = tr.at[g, 1 - yh if other else yh, c, x]
        return remote(mine, mine, xs.at[g, other, k - 1], xr.at[g, other, k - 1], xdev(k))

    def ccopy(g, other):
        mine = tr.at[g, 1 - yh if other else yh, c]
        return remote(mine, mine, cs.at[g, other], cr.at[g, other], cdev)

    def settle():
        nonlocal pair_energy, weight
        loads[2].wait()
        row_line = ve_ref[pl.ds(lax.div(fit, 2), 1), :]
        lanes = lax.broadcasted_iota(jnp.int32, (ROWS, 128), 1)
        wanted = lax.broadcasted_iota(jnp.int32, (ROWS, 128), 0) + lax.rem(fit, 2) * ROWS
        row_energy = jnp.sum(jnp.where(lanes == wanted, row_line, 0.0), axis=1, keepdims=True)
        pair_energy = row_energy + ve_ref[pl.ds(pair, 1), :]
        for load in loads[3:6]:
            load.wait()
        weight = []
        for j in range(NJ):
            line = []
            for k in range(NCFG):
                total = jnp.float32(0.0)
                for n in range(NTERM):
                    total = total + jnp.where(cfg_ref[j, n] == k, cp_ref[j, n], jnp.float32(0.0))
                line.append(total)
            weight.append(line)

    pair_energy, weight = None, None

    def trial(g):
        (yjoin if g == RING else wjoin)()
        denominator = jnp.concatenate([pair_energy - ie_ref[j] for j in GROUPS[g]], axis=1)
        tr[g, yh, c, x] = (ker[g] / denominator).astype(jnp.bfloat16)
        start(hcopy(g))
        for k in (2, 1, 3):
            start(xcopy(g, 0, k))

    def spread(g):
        hcopy(g).wait_recv()
        for k in (2, 1, 3):
            start(xcopy(g, 1, k))
        for k in (1, 3, 2):
            xcopy(g, 0, k).wait_recv()
        start(ccopy(g, 0))

    def swap(g):
        for k in (1, 3, 2):
            xcopy(g, 1, k).wait_recv()
        start(ccopy(g, 1))

    def products(g, other):
        ccopy(g, other).wait_recv()
        sums = [jnp.zeros((2 * ROWS, WIDE), jnp.float32) for _ in range(NCFG // 2)]
        ph = 1 - yh if other else yh
        for px in range(NX):
            pieces = [tr[g, ph, pc, px] for pc in range(NC)]
            both = jnp.concatenate(
                [
                    jnp.concatenate([piece[:, i * COLS : (i + 1) * COLS] for piece in pieces], axis=1)
                    for i in range(2)
                ],
                axis=0,
            )
            rows = pl.ds(pl.multiple_of((px * NYH + ph) * WIDE, WIDE), WIDE)
            for k in range(NCFG // 2):
                pair_of = jnp.concatenate([amp[2 * k, rows], amp[2 * k + 1, rows]], axis=1)
                sums[k] += jnp.dot(both, pair_of, preferred_element_type=jnp.float32)
        for i, j in enumerate(GROUPS[g]):
            cols = slice(i * COLS, (i + 1) * COLS)
            value = ker[g][:, cols]
            for k in range(NCFG):
                part = sums[k // 2][i * ROWS : (i + 1) * ROWS, (k % 2) * COLS : (k % 2 + 1) * COLS]
                value = value + weight[j][k] * part
            if other:
                out_ref[j] = value.astype(jnp.bfloat16)
            else:
                ker[g, :, cols] = value

    pl.semaphore_wait(barrier, len(near + far) + 1)
    greet(0)
    def drain():
        for copy in sent:
            copy.wait_send()
        sent.clear()

    steps = {
        "r": greeted, "z": zsend, "l": zlast, "b": bsend, "a": lambda k: start(acopy(k)), "ax": axsend,
        "ac": acsend, "w": wsend, "t": trial, "s": spread, "c": swap, "f": products, "T": turn, "p": prepare, "d": drain, "wd": wdone, "m": settle,
    }
    for step in ORDER:
        if step[0] == "f" and loads:
            loads.pop().wait()
            loads.clear()
        steps[step[0]](*step[1:])
    drain()


def shards(left, right, virtual_energy, internal_energy, amplitudes, cfg_map, coupling):
    dma = pltpu.SemaphoreType.DMA
    bf16, f32 = jnp.bfloat16, jnp.float32
    out = pl.pallas_call(
        kernel,
        out_shape=pltpu.VMEM((NJ, ROWS, COLS), bf16),
        in_specs=[pl.BlockSpec(memory_space=pl.ANY)] * 7,
        out_specs=pl.BlockSpec(memory_space=pltpu.VMEM),
        scratch_shapes=[
            pltpu.VMEM(left.shape, bf16),
            pltpu.VMEM((left.shape[0], NJ, COLS), bf16),
            pltpu.VMEM((V // 128, 128), f32),
            pltpu.SMEM((NJ,), f32),
            pltpu.SMEM((NJ, NTERM), jnp.int32),
            pltpu.SMEM((NJ, NTERM), f32),
            pltpu.VMEM((NCFG, V, COLS), bf16),
            pltpu.VMEM((NYL, NZ, ROWS, KPAD), bf16),
            pltpu.VMEM((2, KPAD, WIDE), bf16),
            pltpu.VMEM((NZ, NYL, ROWS, WIDE), f32),
            pltpu.VMEM((2, NYL, HALF, ROWS, WIDE), bf16),
            pltpu.VMEM((2, NYL, HALF, ROWS, WIDE), bf16),
            pltpu.VMEM((NYL - 1, ROWS, WIDE), bf16),
            pltpu.VMEM((NYL - 1, ROWS, WIDE), bf16),
            pltpu.VMEM((6, KPAD, WIDE), bf16),
            pltpu.VMEM((3, NC, NX, ROWS, KPAD), bf16),
            pltpu.VMEM((NZ, ROWS, WIDE), f32),
            pltpu.VMEM((NZ, ROWS, WIDE), bf16),
            pltpu.VMEM((NZ, ROWS, WIDE), bf16),
            pltpu.VMEM((2, ROWS, WIDE), f32),
            pltpu.VMEM((2, NYH, NC, NX, ROWS, WIDE), bf16),
            dma((7,)),
            pltpu.SemaphoreType.REGULAR((3,)),
            dma((2, NYL, HALF)),
            dma((2, NYL, HALF)),
            dma((3,)),
            dma((3,)),
            dma((2, 3, 2)),
            dma((2, 3, 2)),
            dma((3,)),
            dma((3,)),
            dma((2, 3)),
            dma((2, 3)),
            dma((2,)),
            dma((2,)),
            dma((NZ,)),
            dma((NZ,)),
            dma((2,)),
            dma((2,)),
            dma((2, 2, 3)),
            dma((2, 2, 3)),
            dma((2, 2)),
            dma((2, 2)),
        ],
        compiler_params=pltpu.CompilerParams(
            collective_id=0, has_side_effects=True, vmem_limit_bytes=56 << 20
        ),
        name="exchange",
    )(left, jnp.transpose(right, (1, 0, 2)), virtual_energy.reshape(V // 128, 128), internal_energy, cfg_map, coupling, amplitudes)
    return jnp.transpose(out, (1, 0, 2))


def solution(mesh):
    placed = (P("fit", None), P(None, "fit", "pair"), P(), P(), P(None, None, "pair"), P(), P())
    return jax.shard_map(
        shards, mesh=mesh, in_specs=placed, out_specs=P("fit", None, "pair"), check_vma=False
    )
```

```python
import jax
import jax.numpy as jnp
from jax import lax
from jax.experimental import pallas as pl
from jax.experimental.pallas import tpu as pltpu
from jax.sharding import PartitionSpec as P

MESH = pl.DeviceIdType.MESH
NX, NYL, NYH, NZ, NC = 4, 4, 2, 8, 2
NY = NYL * NYH
NJ, NTERM, NCFG = 4, 8, 4
ROWS, COLS, V, KPAD = 64, 128, 2048, 256
HALF = NZ // 2
GROUPS = ((0, 1), (2, 3))
RING, GATHER = 0, 1
WIDE = 2 * COLS
RELAY = True
ORDER = (
    ('T',), ('a', 0), ('a', 1), ('p', 4), ('p', 3), ('p', 5), ('z', 3, 0, 0), ('z', 3, 1, 0), ('z', 2, 0, 0),
    ('z', 2, 1, 0), ('z', 1, 0, 0), ('z', 1, 1, 0), ('z', 0, 0, 0), ('z', 0, 1, 0), ('b', 0, 0, 0),
    ('b', 0, 1, 0), ('b', 1, 0, 0), ('b', 1, 1, 0), ('r', 0), ('a', 2), ('p', 2), ('p', 6), ('p', 1),
    ('p', 7), ('p', 0), ('ax', 0), ('z', 3, 0, 1), ('z', 3, 1, 1), ('z', 2, 0, 1), ('z', 2, 1, 1),
    ('z', 1, 0, 1), ('z', 1, 1, 1), ('z', 0, 0, 1), ('z', 0, 1, 1), ('b', 0, 0, 1), ('b', 0, 1, 1),
    ('b', 1, 0, 1), ('b', 1, 1, 1), ('m',), ('r', 1), ('ax', 1), ('z', 3, 0, 2), ('z', 3, 1, 2),
    ('z', 2, 0, 2), ('z', 2, 1, 2), ('z', 1, 0, 2), ('z', 1, 1, 2), ('z', 0, 0, 2), ('z', 0, 1, 2), ('ac', 0),
    ('b', 0, 0, 2), ('b', 0, 1, 2), ('b', 1, 0, 2), ('b', 1, 1, 2), ('r', 2), ('z', 3, 1, 3), ('z', 2, 0, 3),
    ('z', 1, 1, 3), ('z', 0, 0, 3), ('ac', 1), ('l', 3), ('w',), ('l', 2), ('l', 1), ('l', 0), ('t', 0),
    ('t', 1), ('wd',), ('d',), ('s', 0), ('s', 1), ('f', 0, 0), ('c', 0), ('f', 1, 0), ('c', 1), ('d',),
    ('f', 0, 1), ('f', 1, 1),
)


def place(x, yh, yl, z, c):
    return (yl * NZ + z, x * (NYH * NC) + yh * NC + c)


def kernel(
    left_hbm, right_hbm, ve_hbm, ie_hbm, cfg_hbm, cp_hbm, amp_hbm, out_ref,
    left_ref, right_ref, ve_ref, ie_ref, cfg_ref, cp_ref, amp, at, bt,
    pre, zin, zout, tot, yin, bin_, ain, csum, cout, cin, ker, tr,
    in_sem, relay, zs, zr, ys, yr, bs, br, as_, ar, axs, axr, acs, acr, ws, wr, hs, hr, xs, xr, cs, cr,
):
    fit, pair = lax.axis_index("fit"), lax.axis_index("pair")
    z, yl = lax.rem(fit, NZ), lax.div(fit, NZ)
    c, yh, x = lax.rem(pair, NC), lax.rem(lax.div(pair, NC), NYH), lax.div(pair, NYH * NC)
    y = yh * NYL + yl

    def zdev(k):
        return place(x, yh, yl, lax.rem(z + k + NZ, NZ), c)

    def ydev(k):
        return place(x, yh, lax.rem(yl + k + NYL, NYL), z, c)

    def around(k):
        other = lax.rem(y + k + NY, NY)
        return place(x, lax.div(other, NYL), lax.rem(other, NYL), z, c)

    def xdev(k):
        return place(lax.rem(x + k + NX, NX), yh, yl, z, c)

    hdev = place(x, 1 - yh, yl, z, c)
    cdev = place(x, yh, yl, z, 1 - c)

    barrier = pltpu.get_barrier_semaphore()
    near = [zdev(1), zdev(-1), around(1), around(-1), xdev(1), xdev(-1)]
    far = [] if RELAY else (
        [zdev(k) for k in range(2, 7)] + [around(k) for k in range(2, 7)] + [xdev(2)]
    )
    for d in near + far + [cdev]:
        pl.semaphore_signal(barrier, inc=1, device_id=d, device_id_type=MESH)

    loads = [
        pltpu.make_async_copy(source, target, in_sem.at[i])
        for i, (source, target) in enumerate(
            [
                (right_hbm, right_ref), (left_hbm, left_ref), (ve_hbm, ve_ref), (ie_hbm, ie_ref),
                (cfg_hbm, cfg_ref), (cp_hbm, cp_ref), (amp_hbm, amp),
            ]
        )
    ]
    for load in loads[:-1]:
        load.start()

    sent = []

    def start(copy):
        copy.start()
        sent.append(copy)

    def remote(source, target, send, recv, device):
        return pltpu.make_async_remote_copy(
            src_ref=source, dst_ref=target, send_sem=send, recv_sem=recv, device_id=device, device_id_type=MESH
        )

    def greet(r):
        if RELAY:
            for d in near:
                pl.semaphore_signal(relay.at[r], inc=1, device_id=d, device_id_type=MESH)

    def greeted(r):
        if RELAY:
            pl.semaphore_wait(relay.at[r], len(near))
            if r < 2:
                greet(r + 1)

    depth = left_ref.shape[0]
    at[:, :, :, KPAD - 128 :] = jnp.zeros((NYL, NZ, ROWS, 128), jnp.bfloat16)
    bt[:, KPAD - 16 :, :] = jnp.zeros((2, 16, WIDE), jnp.bfloat16)
    loads[0].wait()
    for g, group in enumerate(GROUPS):
        for i, j in enumerate(group):
            bt[g, :depth, i * COLS : (i + 1) * COLS] = right_ref[:, j, :]

    def turn():
        loads[1].wait()
        for m in range(V // 128):
            piece = left_ref[:, m * 128 : (m + 1) * 128].T
            for s in range(2):
                block = 2 * m + s
                at[block // NZ, block % NZ, :, :depth] = piece[s * ROWS : (s + 1) * ROWS]
        loads[-1].start()

    def prepare(k):
        owner = lax.rem(z + k, NZ)
        rows = at[:, owner].reshape(NYL * ROWS, KPAD)
        value = jnp.dot(rows, bt[RING], preferred_element_type=jnp.float32)
        pre[owner] = value.reshape(NYL, ROWS, WIDE)

    def chunk(owner, u):
        return pre[owner, lax.rem(yl + u, NYL)]

    def reach(u, d):
        return HALF if (u + d) % 2 == 0 else HALF - 1

    def owner_at(d, k):
        return lax.rem(z + (k if d == 0 else NZ - k), NZ)

    def zcopy(u, d, h):
        return remote(
            zout.at[d, u, h], zin.at[d, u, h], zs.at[d, u, h], zr.at[d, u, h], zdev(1 if d == 0 else -1)
        )

    def zsend(u, d, h):
        value = chunk(owner_at(d, reach(u, d) - h), u)
        if h > 0:
            zcopy(u, d, h - 1).wait_recv()
            value = value + zin[d, u, h - 1].astype(jnp.float32)
        zout[d, u, h] = value.astype(jnp.bfloat16)
        start(zcopy(u, d, h))

    def ycopy(u):
        return remote(tot.at[u - 1], yin.at[u - 1], ys.at[u - 1], yr.at[u - 1], ydev(u))

    def zlast(u):
        value = chunk(z, u)
        for d in range(2):
            h = reach(u, d) - 1
            zcopy(u, d, h).wait_recv()
            value = value + zin[d, u, h].astype(jnp.float32)
        if u == 0:
            ker[RING] = value
        else:
            tot[u - 1] = value.astype(jnp.bfloat16)
            start(ycopy(u))

    def bcopy(i, d, h):
        part = pl.ds(i * KPAD // 2, KPAD // 2)
        source = bt.at[GATHER, part] if h == 0 else bin_.at[d * 3 + h - 1, part]
        return remote(
            source, bin_.at[d * 3 + h, part], bs.at[d, h, i], br.at[d, h, i], around(1 if d == 0 else -1)
        )

    def bsend(i, d, h):
        if h > 0:
            bcopy(i, d, h - 1).wait_recv()
        start(bcopy(i, d, h))

    def acopy(k):
        step = (1, -1, 2 - 4 * c)[k]
        return remote(
            at.at[lax.rem(yl + step + NYL, NYL), c * NX + x], ain.at[k, c, x], as_.at[k], ar.at[k], around(step)
        )

    batches = ((0, 2), (2, 1))

    def axcopy(part, k):
        some = ain.at[pl.ds(*batches[part]), c, x]
        return remote(some, some, axs.at[part, k - 1], axr.at[part, k - 1], xdev(k))

    def axsend(part):
        first, count = batches[part]
        for k in range(first, first + count):
            acopy(k).wait_recv()
        for k in (2, 1, 3):
            start(axcopy(part, k))

    def accopy(part):
        some = ain.at[pl.ds(*batches[part]), c]
        return remote(some, some, acs.at[part], acr.at[part], cdev)

    def acsend(part):
        for k in (1, 3, 2):
            axcopy(part, k).wait_recv()
        start(accopy(part))

    def wcopy(owner):
        slot_of = lax.rem(owner + NZ - 1 - z, NZ)
        return remote(
            cout.at[owner], cin.at[slot_of], ws.at[slot_of], wr.at[slot_of], place(x, yh, yl, owner, c)
        )

    def wsend():
        low, top, mid = 5 * (1 - lax.div(yl + 3, NYL)), 3 - lax.div(yl + 1, NYL), 4 - 3 * lax.div(yl + 2, NYL)
        for i in range(2):
            for d in range(2):
                bcopy(i, d, 2).wait_recv()
        for part in range(2):
            accopy(part).wait_recv()
        columns = [bt[GATHER]] + [bin_[slot_of] for slot_of in (low, top, mid)]
        for part in range(2):
            rows = [at[yl, part * HALF : (part + 1) * HALF]] + [ain[s, part] for s in range(3)]
            value = sum(
                jnp.dot(a.reshape(HALF * ROWS, KPAD), b, preferred_element_type=jnp.float32)
                for a, b in zip(rows, columns)
            ).reshape(HALF, ROWS, WIDE)
            csum[part * HALF : (part + 1) * HALF] = value
            cout[part * HALF : (part + 1) * HALF] = value.astype(jnp.bfloat16)
            for owner in range(part * HALF, (part + 1) * HALF):

                @pl.when(z != owner)
                def _():
                    wcopy(owner).start()

    def wdone():
        for owner in range(NZ):

            @pl.when(z != owner)
            def _():
                wcopy(owner).wait_send()

    def wjoin():
        value = csum[z]
        for k in (1, 7, 2, 6, 3, 5, 4):
            remote(cout.at[0], cin.at[k - 1], ws.at[k - 1], wr.at[k - 1], zdev(-k)).wait_recv()
            value = value + cin[k - 1].astype(jnp.float32)
        ker[GATHER] = value

    def yjoin():
        value = ker[RING]
        for k in (1, 2, 3):
            ycopy(k).wait_recv()
            value = value + yin[k - 1].astype(jnp.float32)
        ker[RING] = value

    def hcopy(g):
        mine = tr.at[g, yh, c, x]
        return remote(mine, mine, hs.at[g], hr.at[g], hdev)

    def xcopy(g, other, k):
        mine = tr.at[g, 1 - yh if other else yh, c, x]
        return remote(mine, mine, xs.at[g, other, k - 1], xr.at[g, other, k - 1], xdev(k))

    def ccopy(g, other):
        mine = tr.at[g, 1 - yh if other else yh, c]
        return remote(mine, mine, cs.at[g, other], cr.at[g, other], cdev)

    def settle():
        nonlocal pair_energy, weight
        loads[2].wait()
        row_line = ve_ref[pl.ds(lax.div(fit, 2), 1), :]
        lanes = lax.broadcasted_iota(jnp.int32, (ROWS, 128), 1)
        wanted = lax.broadcasted_iota(jnp.int32, (ROWS, 128), 0) + lax.rem(fit, 2) * ROWS
        row_energy = jnp.sum(jnp.where(lanes == wanted, row_line, 0.0), axis=1, keepdims=True)
        pair_energy = row_energy + ve_ref[pl.ds(pair, 1), :]
        for load in loads[3:6]:
            load.wait()
        weight = []
        for j in range(NJ):
            line = []
            for k in range(NCFG):
                total = jnp.float32(0.0)
                for n in range(NTERM):
                    total = total + jnp.where(cfg_ref[j, n] == k, cp_ref[j, n], jnp.float32(0.0))
                line.append(total)
            weight.append(line)

    pair_energy, weight = None, None

    def trial(g):
        (yjoin if g == RING else wjoin)()
        denominator = jnp.concatenate([pair_energy - ie_ref[j] for j in GROUPS[g]], axis=1)
        tr[g, yh, c, x] = (ker[g] / denominator).astype(jnp.bfloat16)
        start(hcopy(g))
        for k in (2, 1, 3):
            start(xcopy(g, 0, k))

    def spread(g):
        hcopy(g).wait_recv()
        for k in (2, 1, 3):
            start(xcopy(g, 1, k))
        for k in (1, 3, 2):
            xcopy(g, 0, k).wait_recv()
        start(ccopy(g, 0))

    def swap(g):
        for k in (1, 3, 2):
            xcopy(g, 1, k).wait_recv()
        start(ccopy(g, 1))

    def products(g, other):
        ccopy(g, other).wait_recv()
        sums = [jnp.zeros((2 * ROWS, WIDE), jnp.float32) for _ in range(NCFG // 2)]
        ph = 1 - yh if other else yh
        for px in range(NX):
            pieces = [tr[g, ph, pc, px] for pc in range(NC)]
            both = jnp.concatenate(
                [
                    jnp.concatenate([piece[:, i * COLS : (i + 1) * COLS] for piece in pieces], axis=1)
                    for i in range(2)
                ],
                axis=0,
            )
            rows = pl.ds(pl.multiple_of((px * NYH + ph) * WIDE, WIDE), WIDE)
            for k in range(NCFG // 2):
                pair_of = jnp.concatenate([amp[2 * k, rows], amp[2 * k + 1, rows]], axis=1)
                sums[k] += jnp.dot(both, pair_of, preferred_element_type=jnp.float32)
        for i, j in enumerate(GROUPS[g]):
            cols = slice(i * COLS, (i + 1) * COLS)
            value = ker[g][:, cols]
            for k in range(NCFG):
                part = sums[k // 2][i * ROWS : (i + 1) * ROWS, (k % 2) * COLS : (k % 2 + 1) * COLS]
                value = value + weight[j][k] * part
            if other:
                out_ref[j] = value.astype(jnp.bfloat16)
            else:
                ker[g, :, cols] = value

    pl.semaphore_wait(barrier, len(near + far) + 1)
    greet(0)
    def drain():
        for copy in sent:
            copy.wait_send()
        sent.clear()

    steps = {
        "r": greeted, "z": zsend, "l": zlast, "b": bsend, "a": lambda k: start(acopy(k)), "ax": axsend,
        "ac": acsend, "w": wsend, "t": trial, "s": spread, "c": swap, "f": products, "T": turn, "p": prepare, "d": drain, "wd": wdone, "m": settle,
    }
    for step in ORDER:
        if step[0] == "f" and loads:
            loads.pop().wait()
            loads.clear()
        steps[step[0]](*step[1:])
    drain()


def shards(left, right, virtual_energy, internal_energy, amplitudes, cfg_map, coupling):
    dma = pltpu.SemaphoreType.DMA
    bf16, f32 = jnp.bfloat16, jnp.float32
    out = pl.pallas_call(
        kernel,
        out_shape=pltpu.VMEM((NJ, ROWS, COLS), bf16),
        in_specs=[pl.BlockSpec(memory_space=pl.ANY)] * 7,
        out_specs=pl.BlockSpec(memory_space=pltpu.VMEM),
        scratch_shapes=[
            pltpu.VMEM(left.shape, bf16),
            pltpu.VMEM((left.shape[0], NJ, COLS), bf16),
            pltpu.VMEM((V // 128, 128), f32),
            pltpu.SMEM((NJ,), f32),
            pltpu.SMEM((NJ, NTERM), jnp.int32),
            pltpu.SMEM((NJ, NTERM), f32),
            pltpu.VMEM((NCFG, V, COLS), bf16),
            pltpu.VMEM((NYL, NZ, ROWS, KPAD), bf16),
            pltpu.VMEM((2, KPAD, WIDE), bf16),
            pltpu.VMEM((NZ, NYL, ROWS, WIDE), f32),
            pltpu.VMEM((2, NYL, HALF, ROWS, WIDE), bf16),
            pltpu.VMEM((2, NYL, HALF, ROWS, WIDE), bf16),
            pltpu.VMEM((NYL - 1, ROWS, WIDE), bf16),
            pltpu.VMEM((NYL - 1, ROWS, WIDE), bf16),
            pltpu.VMEM((6, KPAD, WIDE), bf16),
            pltpu.VMEM((3, NC, NX, ROWS, KPAD), bf16),
            pltpu.VMEM((NZ, ROWS, WIDE), f32),
            pltpu.VMEM((NZ, ROWS, WIDE), bf16),
            pltpu.VMEM((NZ, ROWS, WIDE), bf16),
            pltpu.VMEM((2, ROWS, WIDE), f32),
            pltpu.VMEM((2, NYH, NC, NX, ROWS, WIDE), bf16),
            dma((7,)),
            pltpu.SemaphoreType.REGULAR((3,)),
            dma((2, NYL, HALF)),
            dma((2, NYL, HALF)),
            dma((3,)),
            dma((3,)),
            dma((2, 3, 2)),
            dma((2, 3, 2)),
            dma((3,)),
            dma((3,)),
            dma((2, 3)),
            dma((2, 3)),
            dma((2,)),
            dma((2,)),
            dma((NZ,)),
            dma((NZ,)),
            dma((2,)),
            dma((2,)),
            dma((2, 2, 3)),
            dma((2, 2, 3)),
            dma((2, 2)),
            dma((2, 2)),
        ],
        compiler_params=pltpu.CompilerParams(
            collective_id=0, has_side_effects=True, vmem_limit_bytes=56 << 20
        ),
        name="exchange",
    )(left, jnp.transpose(right, (1, 0, 2)), virtual_energy.reshape(V // 128, 128), internal_energy, cfg_map, coupling, amplitudes)
    return jnp.transpose(out, (1, 0, 2))


def solution(mesh):
    placed = (P("fit", None), P(None, "fit", "pair"), P(), P(), P(None, None, "pair"), P(), P())
    return jax.shard_map(
        shards, mesh=mesh, in_specs=placed, out_specs=P("fit", None, "pair"), check_vma=False
    )
```
